256 devices in a mesh: expert: 2 (over core), hidden: 32 (over x, z), replica: 4 (over y).
Axes of the slice: x: 4, y: 4, z: 8, core: 2. Of those that a mesh axis runs over, the one named last changes fastest.
Arguments:
- activations: bfloat16 [2, 4096, 4096], P('expert', 'replica', 'hidden'), may hold values from -6 to 6
- hidden_grad: bfloat16 [2, 4096, 14336], P('expert', 'replica', 'hidden'), may hold values from -0.1875 to 0.1875
- error_buffer: bfloat16 [2, 4, 4096, 14336], P('expert', 'replica', None, 'hidden'), may hold values from -4 to 4
- q_previous: float32 [2, 14336, 32], P('expert', 'hidden'), may hold values from -0.046875 to 0.046875
Outputs:
- p_factor: float32 [2, 4096, 32], P('expert')
- q_factor: float32 [2, 14336, 32], P('expert', 'hidden')
- new_error: bfloat16 [2, 4, 4096, 14336], P('expert', 'replica', None, 'hidden')
The draws below stay inside these ranges and needn't reach their ends.
All inputs are finite; a program needn't handle non-finite values.
Results may differ from the reference program's by a relative error of at most 0.0055.
Values may be sent and summed in bfloat16 or wider, within the bound.
No kernel may reach another device: no remote copies, remote signals or barrier semaphores. Data moves between devices by JAX's collectives and lax.ppermute only.
A program may use at most 64 MiB of HBM per device.

```python
import jax
import jax.numpy as jnp
from jax import lax

D = 4096
FF = 14336
RANK = 32
TOK_DEV = 1024
EXPERTS = 2
TOKENS = 4096
N_REPLICA = 4


def shard_levels(stream_key, dims, shards, least, high):
    factor_of = 1.0
    for position, shards_of in shards:
        heights = jax.random.uniform(jax.random.fold_in(jax.random.fold_in(stream_key, 6), position), (shards_of,), jnp.float32, least / len(shards), high / len(shards))
        factor_of = factor_of * jnp.repeat(jnp.exp(heights), dims[position] // shards_of).reshape((-1,) + (1,) * (len(dims) - 1 - position))
    return factor_of


def noise(key, dims, spread, limit, pieces=(), kind=jnp.bfloat16):
    drawn = jax.random.normal(key, dims, jnp.float32) * spread
    if len(pieces) > 0:
        drawn = shard_levels(key, dims, pieces, -0.22, 0.18) * drawn
    return jnp.clip(drawn, min=-limit, max=limit).astype(kind)


def setup_inputs(seed: int = 0) -> dict:
    key_list = jax.random.split(jax.random.key(seed), 5)
    activations = noise(key_list[0], (EXPERTS, TOKENS, D), 1.0, 6.0, ((0, 2), (1, 4), (2, 32)))
    hidden_grad = noise(key_list[1], (EXPERTS, TOKENS, FF), TOK_DEV ** -0.5, 0.1875, ((0, 2), (1, 4), (2, 32)))
    error_buffer = noise(key_list[2], (EXPERTS, N_REPLICA, D, FF), 0.5, 4.0, ((0, 2), (1, 4), (3, 32)))
    q_previous = noise(key_list[3], (EXPERTS, FF, RANK), FF ** -0.5, 0.046875, ((0, 2), (1, 32)), jnp.float32)
    return dict(activations=activations, hidden_grad=hidden_grad, error_buffer=error_buffer, q_previous=q_previous)


def orthonormal(p_sum):
    gram_matrix = jnp.dot(p_sum.T.astype(jnp.float32), p_sum.astype(jnp.float32), precision=lax.Precision.HIGHEST, preferred_element_type=jnp.float32)
    lower_tri = jnp.linalg.cholesky(gram_matrix)
    return jax.scipy.linalg.solve_triangular(lower_tri, p_sum.T, lower=True).T

def reference(activations, hidden_grad, error_buffer, q_previous):
    p_list = []
    q_list = []
    err_list = []
    for expert_id in range(EXPERTS):
        q_low = q_previous[expert_id].astype(jnp.bfloat16)
        corrected_list = []
        p_sum = jnp.zeros((D, RANK), jnp.float32)
        for rep in range(N_REPLICA):
            inputs = activations[expert_id, rep * TOK_DEV:(rep + 1) * TOK_DEV]
            cotangent = hidden_grad[expert_id, rep * TOK_DEV:(rep + 1) * TOK_DEV]
            gradient = jnp.dot(inputs.T.astype(jnp.float32), cotangent.astype(jnp.float32), preferred_element_type=jnp.float32)
            corrected = (error_buffer[expert_id, rep].astype(jnp.float32) + gradient).astype(jnp.bfloat16)
            corrected_list.append(corrected)
            p_sum = p_sum + jnp.dot(corrected.astype(jnp.float32), q_low.astype(jnp.float32), preferred_element_type=jnp.float32)
        p_sum = p_sum / N_REPLICA
        p_orth = orthonormal(p_sum)
        p_low = p_orth.astype(jnp.bfloat16)
        q_sum = jnp.zeros((FF, RANK), jnp.float32)
        for rep in range(N_REPLICA):
            q_sum = q_sum + jnp.dot(corrected_list[rep].T.astype(jnp.float32), p_low.astype(jnp.float32), preferred_element_type=jnp.float32)
        q_sum = q_sum / N_REPLICA
        q_round = q_sum.astype(jnp.bfloat16)
        approx = jnp.dot(p_low.astype(jnp.float32), q_round.T.astype(jnp.float32), preferred_element_type=jnp.float32)
        errors = [(corrected_list[rep].astype(jnp.float32) - approx).astype(jnp.bfloat16) for rep in range(N_REPLICA)]
        p_list.append(p_orth)
        q_list.append(q_sum)
        err_list.append(jnp.stack(errors))
    return (jnp.stack(p_list), jnp.stack(q_list), jnp.stack(err_list))
```

```python
import jax
import jax.numpy as jnp
from jax import lax
from jax.experimental import pallas as pl
from jax.experimental.pallas import tpu as pltpu
from jax.sharding import PartitionSpec as P

F32 = jnp.float32
BF16 = jnp.bfloat16
VMEM = pl.BlockSpec(memory_space=pltpu.VMEM)
LIMIT = pltpu.CompilerParams(vmem_limit_bytes=48 * 1024 * 1024)
NT = (((1,), (1,)), ((), ()))
TN = (((0,), (0,)), ((), ()))


def split3(v):
    a = v.astype(BF16)
    r = v - a.astype(F32)
    b = r.astype(BF16)
    c = (r - b.astype(F32)).astype(BF16)
    return jnp.concatenate([a, b, c], axis=0)


def fold3(v):
    n = v.shape[0] // 3
    return v[:n] + v[n : 2 * n] + v[2 * n :]


def first_kernel(q_ref, e_ref, h_ref, out_ref):
    q = q_ref[...].astype(BF16)
    eq = jnp.dot(q, e_ref[...], preferred_element_type=F32)
    t = jnp.dot(q, h_ref[...], preferred_element_type=F32)
    for i in range(4):
        out_ref[i, 0:32, :] = eq[:, 128 * i : 128 * (i + 1)]
        out_ref[i, 32:40, :] = t[8 * i : 8 * (i + 1), :]


def first(q_t, e_t, h_t):
    return pl.pallas_call(
        first_kernel,
        grid=(8,),
        in_specs=[
            pl.BlockSpec((32, 448), lambda g: (0, 0)),
            pl.BlockSpec((448, 512), lambda g: (0, g)),
            pl.BlockSpec((448, 128), lambda g: (0, g)),
        ],
        out_specs=pl.BlockSpec((4, 40, 128), lambda g: (g, 0, 0)),
        out_shape=jax.ShapeDtypeStruct((32, 40, 128), F32),
        compiler_params=LIMIT,
        name="eq_hq",
    )(q_t, e_t, h_t)


def split_sum_kernel(r_ref, eq_ref, t_ref):
    s = jnp.sum(r_ref[...], axis=0)
    eq_ref[...] = s[0:32]
    t_ref[...] = jnp.broadcast_to(s[32:40][None], t_ref.shape)


def split_sum(r):
    return pl.pallas_call(
        split_sum_kernel,
        in_specs=[VMEM],
        out_specs=[VMEM, VMEM],
        out_shape=[
            jax.ShapeDtypeStruct((32, 128), F32),
            jax.ShapeDtypeStruct((32, 8, 128), F32),
        ],
        compiler_params=LIMIT,
        name="sum_first",
    )(r)


def tile_sum_kernel(r_ref, t_ref):
    t_ref[...] = jnp.broadcast_to(jnp.sum(r_ref[...], axis=0)[None], t_ref.shape)


def tile_sum(r):
    return pl.pallas_call(
        tile_sum_kernel,
        in_specs=[VMEM],
        out_specs=VMEM,
        out_shape=jax.ShapeDtypeStruct((32, 8, 128), F32),
        compiler_params=LIMIT,
        name="sum_tiles",
    )(r)


def rows_of(t_ref):
    return jnp.concatenate([t_ref[4 * j : 4 * j + 4].reshape(32, 128) for j in range(8)], axis=1)


def slab_kernel(eq_ref, t_ref, x_ref, out_ref):
    t = split3(rows_of(t_ref))
    out_ref[...] = eq_ref[...] + fold3(jnp.dot(t, x_ref[...], preferred_element_type=F32))


def slab(eq, t, x):
    return pl.pallas_call(
        slab_kernel,
        in_specs=[VMEM] * 3,
        out_specs=VMEM,
        out_shape=jax.ShapeDtypeStruct((32, 128), F32),
        compiler_params=LIMIT,
        name="p_slab",
    )(eq, t, x)


def xp_kernel(p_ref, x_ref, out_ref):
    y = lax.dot_general(p_ref[...], x_ref[...], NT, preferred_element_type=F32)
    for j in range(8):
        for i in range(4):
            out_ref[4 * j + i] = y[8 * i : 8 * i + 8, 128 * j : 128 * j + 128]


def xp(p_slab, x):
    return pl.pallas_call(
        xp_kernel,
        in_specs=[VMEM] * 2,
        out_specs=VMEM,
        out_shape=jax.ShapeDtypeStruct((32, 8, 128), F32),
        compiler_params=LIMIT,
        name="x_p",
    )(p_slab, x)


def q_kernel(p_ref, y_ref, e_ref, h_ref, out_ref):
    y = split3(rows_of(y_ref))
    part = lax.dot_general(p_ref[...], e_ref[...], NT, preferred_element_type=F32)
    out_ref[...] = part + fold3(lax.dot_general(y, h_ref[...], NT, preferred_element_type=F32))


def q_part(p_low, y, e_t, h_t):
    return pl.pallas_call(
        q_kernel,
        in_specs=[VMEM] * 4,
        out_specs=VMEM,
        out_shape=jax.ShapeDtypeStruct((32, 448), F32),
        compiler_params=LIMIT,
        name="q_part",
    )(p_low, y, e_t, h_t)


def final_kernel(x_ref, h_ref, e_ref, p_ref, q_ref, out_ref):
    q = q_ref[...].astype(BF16)
    for c in range(2):
        cols = slice(256 * c, 256 * (c + 1))
        x = jnp.concatenate([x_ref[2 * c], x_ref[2 * c + 1]], axis=1)
        grad = jnp.dot(h_ref[...], x, preferred_element_type=F32)
        corrected = (e_ref[:, cols].astype(F32) + grad).astype(BF16)
        approx = lax.dot_general(q, p_ref[:, cols], TN, preferred_element_type=F32)
        out_ref[:, cols] = (corrected.astype(F32) - approx).astype(BF16)


def final(x_all, h_t, e_t, p_low, q_t):
    return pl.pallas_call(
        final_kernel,
        grid=(8,),
        in_specs=[
            pl.BlockSpec((4, 1024, 128), lambda g: (g, 0, 0)),
            pl.BlockSpec((448, 1024), lambda g: (0, 0)),
            pl.BlockSpec((448, 512), lambda g: (0, g)),
            pl.BlockSpec((32, 512), lambda g: (0, g)),
            pl.BlockSpec((32, 448), lambda g: (0, 0)),
        ],
        out_specs=pl.BlockSpec((448, 512), lambda g: (0, g)),
        out_shape=jax.ShapeDtypeStruct((448, 4096), BF16),
        compiler_params=LIMIT,
        name="new_error",
    )(x_all, h_t, e_t, p_low, q_t)


def swap(v):
    return lax.all_to_all(v, "hidden", 0, 0)


def sum_replicas(v):
    others = [lax.ppermute(v, "replica", [(i, (i + s) % 4) for i in range(4)]) for s in (1, 3, 2)]
    return v + others[0] + others[1] + others[2]


def shards(activations, hidden_grad, error_buffer, q_previous):
    x = activations[0]
    h_t = hidden_grad[0].T
    e_t = error_buffer[0, 0].T
    q_t = q_previous[0].T
    x_all = lax.all_gather(x, "hidden", axis=0)
    eq, t = split_sum(swap(first(q_t, e_t, h_t)))
    p_slab = sum_replicas(slab(eq, swap(t), x)) * 0.25
    p_sum = swap(jnp.broadcast_to(p_slab[None], (32, 32, 128)))
    p_sum = p_sum.transpose(1, 0, 2).reshape(32, 4096)
    gram = lax.dot_general(
        p_sum, p_sum, NT, precision=lax.Precision.HIGHEST, preferred_element_type=F32
    )
    p_factor = jax.scipy.linalg.solve_triangular(jnp.linalg.cholesky(gram), p_sum, lower=True)
    p_low = p_factor.astype(BF16)
    own = lax.dynamic_slice(p_low, (0, lax.axis_index("hidden") * 128), (32, 128))
    y = swap(tile_sum(swap(xp(own, x))))
    q_factor = sum_replicas(q_part(p_low, y, e_t, h_t)) * 0.25
    new_error = final(x_all, h_t, e_t, p_low, q_factor)
    return (p_factor.T[None], q_factor.T[None], new_error.T[None, None])


def solution(mesh):
    in_specs = (
        P("expert", "replica", "hidden"),
        P("expert", "replica", "hidden"),
        P("expert", "replica", None, "hidden"),
        P("expert", "hidden", None),
    )
    out_specs = (
        P("expert", None, None),
        P("expert", "hidden", None),
        P("expert", "replica", None, "hidden"),
    )
    return jax.shard_map(shards, mesh=mesh, in_specs=in_specs, out_specs=out_specs, check_vma=False)
```

```python
import functools

import jax
import jax.numpy as jnp
from jax import lax
from jax.experimental import pallas as pl
from jax.experimental.pallas import tpu as pltpu
from jax.sharding import PartitionSpec as P

F32 = jnp.float32
BF16 = jnp.bfloat16
VMEM = pl.BlockSpec(memory_space=pltpu.VMEM)
SMEM = pl.BlockSpec(memory_space=pltpu.SMEM)


def vmem(mib):
    return pltpu.CompilerParams(vmem_limit_bytes=mib * 1024 * 1024)

NT = (((1,), (1,)), ((), ()))
TN = (((0,), (0,)), ((), ()))
SOURCE_Z = (0, -1, 1, -2, 2, -3, 3, 4)


def split3(v):
    a = v.astype(BF16)
    r = v - a.astype(F32)
    b = r.astype(BF16)
    c = (r - b.astype(F32)).astype(BF16)
    return jnp.concatenate([a, b, c], axis=0)


def fold3(v):
    n = v.shape[0] // 3
    return v[:n] + v[n : 2 * n] + v[2 * n :]


def first_kernel(x_ref, q_ref, e_ref, h_ref, *outs):
    q = q_ref[...].astype(BF16)
    t = jnp.dot(q, h_ref[...], preferred_element_type=F32)
    high = t.astype(BF16)
    low = (t - high.astype(F32)).astype(BF16)
    for s, out in enumerate(outs):
        cols = pl.ds(pl.multiple_of((x_ref[0] + s) % 4 * 1024, 1024), 1024)
        eq = jnp.dot(q, e_ref[:, cols], preferred_element_type=F32)
        out[0:32, :] = high
        out[32:64, :] = low
        out[64:96, :] = eq.astype(BF16)


def first(x_index, q_t, e_t, h_t):
    return pl.pallas_call(
        first_kernel,
        in_specs=[SMEM] + [VMEM] * 3,
        out_specs=[VMEM] * 4,
        out_shape=[jax.ShapeDtypeStruct((96, 1024), BF16)] * 4,
        compiler_params=vmem(10),
        name="eq_hq",
    )(x_index, q_t, e_t, h_t)


def column_kernel(z_ref, m0_ref, m1_ref, m2_ref, m3_ref, *refs):
    x_refs, out_ref = refs[:8], refs[8]
    m = sum(r[...].astype(F32) for r in (m0_ref, m1_ref, m2_ref, m3_ref))
    t = split3(m[0:32] + m[32:64])
    eq = m[64:96]
    for j in range(8):
        out_ref[z_ref[j]] = fold3(jnp.dot(t, x_refs[j][...], preferred_element_type=F32))
    for z in range(8):
        out_ref[z] += eq[:, 128 * z : 128 * (z + 1)]


def column(z_index, messages, own):
    return pl.pallas_call(
        column_kernel,
        in_specs=[SMEM] + [VMEM] * 12,
        out_specs=VMEM,
        out_shape=jax.ShapeDtypeStruct((8, 32, 128), F32),
        compiler_params=vmem(8),
        name="p_column",
    )(z_index, *messages, *own)


def add_spread_kernel(scale, in_ref, out_ref):
    s = jnp.sum(in_ref[...], axis=0) * scale
    out_ref[...] = jnp.broadcast_to(s[None], out_ref.shape)


def add_spread(v, copies, scale):
    return pl.pallas_call(
        functools.partial(add_spread_kernel, scale),
        in_specs=[VMEM],
        out_specs=VMEM,
        out_shape=jax.ShapeDtypeStruct((copies, *v.shape[1:]), F32),
        compiler_params=vmem(4),
        name="add_spread",
    )(v)


def pack_kernel(*refs):
    rows = refs[0].shape[0]
    for i, ref in enumerate(refs[:-1]):
        refs[-1][rows * i : rows * (i + 1), :] = ref[...]


def pack(arrays):
    rows = arrays[0].shape[0]
    return pl.pallas_call(
        pack_kernel,
        in_specs=[VMEM] * len(arrays),
        out_specs=VMEM,
        out_shape=jax.ShapeDtypeStruct((rows * len(arrays), 128), BF16),
        compiler_params=vmem(6),
        name="pack",
    )(*arrays)


def correct_kernel(at_ref, h_ref, e_ref, *refs):
    x_refs, out_ref = refs[:-1], refs[-1]
    slabs = [(r, i) for r in x_refs for i in range(r.shape[0] // 1024)]
    for pair in range(len(slabs) // 2):
        two = slabs[2 * pair : 2 * pair + 2]
        x = jnp.concatenate([r[1024 * i : 1024 * (i + 1), :] for r, i in two], axis=1)
        grad = jnp.dot(h_ref[...], x, preferred_element_type=F32)
        for s in range(2):
            cols = pl.ds(pl.multiple_of(at_ref[2 * pair + s], 128), 128)
            both = e_ref[:, cols].astype(F32) + grad[:, 128 * s : 128 * (s + 1)]
            out_ref[:, cols] = both.astype(BF16)


def correct_more_kernel(at_ref, h_ref, e_ref, c_ref, *refs):
    correct_kernel(at_ref, h_ref, e_ref, *refs)


def correct(places, h_t, e_t, arrays, before=None):
    kept = [] if before is None else [before]
    return pl.pallas_call(
        correct_kernel if before is None else correct_more_kernel,
        in_specs=[SMEM] + [VMEM] * (2 + len(kept) + len(arrays)),
        out_specs=VMEM,
        out_shape=jax.ShapeDtypeStruct((448, 4096), BF16),
        input_output_aliases={} if before is None else {3: 0},
        compiler_params=vmem(22),
        name="corrected",
    )(places, h_t, e_t, *kept, *arrays)


def project_kernel(p_ref, c_ref, out_ref):
    p = split3(jnp.concatenate([p_ref[i] for i in range(32)], axis=1))
    out_ref[...] = fold3(lax.dot_general(p, c_ref[...], NT, preferred_element_type=F32))


def project(p_blocks, c_t):
    return pl.pallas_call(
        project_kernel,
        in_specs=[VMEM] * 2,
        out_specs=VMEM,
        out_shape=jax.ShapeDtypeStruct((32, 448), F32),
        compiler_params=vmem(10),
        name="c_p",
    )(p_blocks, c_t)


def factor_kernel(p_ref, inv_ref, p_out_ref, low_ref):
    p = jnp.concatenate([p_ref[i] for i in range(32)], axis=1)
    gram = lax.dot_general(
        p, p, NT, precision=lax.Precision.HIGHEST, preferred_element_type=F32
    )
    row = lax.broadcasted_iota(jnp.int32, (32, 128), 0)
    col = lax.broadcasted_iota(jnp.int32, (32, 128), 1)
    work = jnp.concatenate([gram, jnp.zeros((32, 96), F32)], axis=1)
    work = jnp.where(col == row + 32, 1.0, work)
    scale = jnp.zeros((32, 1), F32)
    for j in range(32):
        pivot = work[j : j + 1, j : j + 1]
        below = jnp.where(row[:, :1] > j, work[:, j : j + 1], 0.0)
        scale = jnp.where(row[:, :1] == j, pivot, scale)
        work = work - below * (work[j : j + 1, :] / pivot)
    inverse = work[:, 32:64] / jnp.sqrt(scale)
    inv_ref[...] = inverse
    out = jnp.dot(inverse, p, precision=lax.Precision.HIGHEST, preferred_element_type=F32)
    p_out_ref[...] = out
    low_ref[...] = out.astype(BF16)


def factor(p_blocks):
    return pl.pallas_call(
        factor_kernel,
        in_specs=[VMEM],
        out_specs=[VMEM] * 3,
        out_shape=[
            jax.ShapeDtypeStruct((32, 32), F32),
            jax.ShapeDtypeStruct((32, 4096), F32),
            jax.ShapeDtypeStruct((32, 4096), BF16),
        ],
        compiler_params=vmem(8),
        name="factor",
    )(p_blocks)


def final_kernel(inv_ref, a_ref, b_ref, c_ref, d_ref, low_ref, cor_ref, q_ref, out_ref, keep):
    @pl.when(pl.program_id(0) == 0)
    def _():
        w = (a_ref[...] + b_ref[...] + c_ref[...] + d_ref[...]) * 0.25
        q = jnp.dot(
            inv_ref[...], w, precision=lax.Precision.HIGHEST, preferred_element_type=F32
        )
        q_ref[...] = q
        keep[...] = q.astype(BF16)

    cols = pl.ds(pl.multiple_of(pl.program_id(0) * 512, 512), 512)
    approx = lax.dot_general(keep[...], low_ref[:, cols], TN, preferred_element_type=F32)
    out_ref[...] = (cor_ref[:, cols].astype(F32) - approx).astype(BF16)


def final(inverse, parts, p_low, c_t):
    whole = lambda *shape: pl.BlockSpec(shape, lambda g: (0, 0))
    return pl.pallas_call(
        final_kernel,
        grid=(8,),
        in_specs=[VMEM] * 7,
        out_specs=[whole(32, 448), pl.BlockSpec((448, 512), lambda g: (0, g))],
        out_shape=[
            jax.ShapeDtypeStruct((32, 448), F32),
            jax.ShapeDtypeStruct((448, 4096), BF16),
        ],
        scratch_shapes=[pltpu.VMEM((32, 448), BF16)],
        compiler_params=vmem(12),
        name="new_error",
    )(inverse, *parts, p_low, c_t)


def swap(v, axis="hidden", groups=None):
    return lax.all_to_all(v, axis, 0, 0, axis_index_groups=groups)


def replicas(v):
    return [v] + [
        lax.ppermute(v, "replica", [(i, (i + s) % 4) for i in range(4)]) for s in (1, 3, 2)
    ]


def move(v, dx, dz):
    pairs = [(h, (h // 8 + dx) % 4 * 8 + (h % 8 + dz) % 8) for h in range(32)]
    return lax.ppermute(v, "hidden", pairs)


def after(v, *before):
    return lax.optimization_barrier((v, *before))[0]


def shards(activations, hidden_grad, error_buffer, q_previous):
    x = activations[0]
    h_t = hidden_grad[0].T
    e_t = error_buffer[0, 0].T
    q_t = q_previous[0].T
    me = lax.axis_index("hidden")
    x_index, z_index = me // 8, me % 8
    z_order = jnp.stack([(z_index + rz) % 8 for rz in SOURCE_Z]).astype(jnp.int32)

    def places(sources):
        order = [(x_index + rx) % 4 * 1024 + z_order * 128 for rx in sources]
        return jnp.concatenate(order).astype(jnp.int32)

    mine, *others = first(x_index.astype(jnp.int32)[None], q_t, e_t, h_t)
    plus, minus = [x, move(x, 0, 1)], [x, move(x, 0, -1)]
    far = move(x, 2, 0)
    messages = [mine] + [move(m, dx, 0) for m, dx in zip(others, (1, 2, -1))]
    plus.append(move(after(plus[1], mine, far), 0, 1))
    minus.append(move(after(minus[1], mine, far), 0, -1))
    f_plus, f_minus = [after(far, plus[2], minus[2])], [after(far, plus[2], minus[2])]
    plus.append(move(plus[2], 0, 1))
    minus.append(move(minus[2], 0, -1))
    last = move(after(plus[3], *messages), 0, 1)
    own = [x, plus[1], minus[1], plus[2], minus[2], plus[3], minus[3], last]
    bundle = after(pack(own[:5]), plus[3], minus[3], *messages)
    near = [move(bundle, 1, 0), move(bundle, -1, 0)]
    bundle = pack(own[5:])
    near += [move(bundle, 1, 0), move(bundle, -1, 0)]
    for _ in range(3):
        f_plus.append(move(f_plus[-1], 0, 1))
        f_minus.append(move(f_minus[-1], 0, -1))
    f_last = move(f_minus[3], 0, -1)
    far = [far, f_plus[1], f_minus[1], f_plus[2], f_minus[2], f_plus[3], f_minus[3], f_last]
    column_groups = [[8 * i + z for z in range(8)] for i in range(4)]
    p_parts = after(column(z_order, messages, own), f_plus[1], f_minus[1])
    p_parts = swap(p_parts, groups=column_groups)
    p_parts = swap(after(add_spread(p_parts, 4, 1.0), f_plus[2], f_minus[2]), "replica")
    p_blocks = swap(after(add_spread(p_parts, 32, 0.25), f_plus[3], f_minus[3]))
    at = places((0, -1, 1, 2))
    at_first = jnp.concatenate([at[0:8], at[24:32]])
    at_second = jnp.concatenate([at[8:13], at[16:21], at[13:16], at[21:24]])
    c_t = correct(at_first, h_t, e_t, [*own, *far])
    c_t = correct(at_second, h_t, e_t, near, c_t)
    parts = replicas(project(p_blocks, c_t))
    inverse, p_factor, p_low = factor(p_blocks)
    q_factor, new_error = final(inverse, parts, p_low, c_t)
    return (p_factor.T[None], q_factor.T[None], new_error.T[None, None])


def solution(mesh):
    in_specs = (
        P("expert", "replica", "hidden"),
        P("expert", "replica", "hidden"),
        P("expert", "replica", None, "hidden"),
        P("expert", "hidden", None),
    )
    out_specs = (
        P("expert", None, None),
        P("expert", "hidden", None),
        P("expert", "replica", None, "hidden"),
    )
    return jax.shard_map(shards, mesh=mesh, in_specs=in_specs, out_specs=out_specs, check_vma=False)
```

```python
import functools

import jax
import jax.numpy as jnp
from jax import lax
from jax.experimental import pallas as pl
from jax.experimental.pallas import tpu as pltpu
from jax.sharding import PartitionSpec as P

F32 = jnp.float32
BF16 = jnp.bfloat16
VMEM = pl.BlockSpec(memory_space=pltpu.VMEM)
SMEM = pl.BlockSpec(memory_space=pltpu.SMEM)
HBM = pl.BlockSpec(memory_space=pltpu.HBM)
ANY = pl.BlockSpec(memory_space=pl.ANY)


def vmem(mib):
    return pltpu.CompilerParams(vmem_limit_bytes=mib * 1024 * 1024)

NT = (((1,), (1,)), ((), ()))
TN = (((0,), (0,)), ((), ()))
SOURCE_Z = (0, -1, 1, -2, 2, -3, 3, 4)


def in_hbm(v):
    return pltpu.with_memory_space_constraint(v, pltpu.HBM)


def in_vmem(v):
    return pltpu.with_memory_space_constraint(v, pltpu.VMEM)


def load_all(pairs, sems):
    copies = [pltpu.make_async_copy(a, b, sems.at[i]) for i, (a, b) in enumerate(pairs)]
    for copy in copies:
        copy.start()
    return copies


def split3(v):
    a = v.astype(BF16)
    r = v - a.astype(F32)
    b = r.astype(BF16)
    c = (r - b.astype(F32)).astype(BF16)
    return jnp.concatenate([a, b, c], axis=0)


def fold3(v):
    n = v.shape[0] // 3
    return v[:n] + v[n : 2 * n] + v[2 * n :]


def first_kernel(x_ref, q_hbm, e_hbm, h_hbm, *refs):
    outs, (q_ref, e_ref, h_ref, sems) = refs[:4], refs[4:]
    columns = [pl.ds(pl.multiple_of((x_ref[0] + s) % 4 * 1024, 1024), 1024) for s in range(4)]
    loads = load_all(
        [(q_hbm, q_ref), (h_hbm, h_ref)]
        + [(e_hbm.at[:, columns[s]], e_ref.at[s]) for s in (1, 3, 2, 0)],
        sems,
    )
    loads[0].wait()
    q = q_ref[...].astype(BF16)
    loads[1].wait()
    t = jnp.dot(q, h_ref[...], preferred_element_type=F32)
    high = t.astype(BF16)
    low = (t - high.astype(F32)).astype(BF16)
    for load, s in zip(loads[2:], (1, 3, 2, 0)):
        load.wait()
        eq = jnp.dot(q, e_ref[s], preferred_element_type=F32)
        outs[s][0:32, :] = high
        outs[s][32:64, :] = low
        outs[s][64:96, :] = eq.astype(BF16)


def first(x_index, q_t, e_t, h_t):
    return pl.pallas_call(
        first_kernel,
        in_specs=[SMEM] + [HBM] * 3,
        out_specs=[VMEM] * 4,
        out_shape=[jax.ShapeDtypeStruct((96, 1024), BF16)] * 4,
        scratch_shapes=[
            pltpu.VMEM((32, 448), F32),
            pltpu.VMEM((4, 448, 1024), BF16),
            pltpu.VMEM((448, 1024), BF16),
            pltpu.SemaphoreType.DMA((6,)),
        ],
        compiler_params=vmem(12),
        name="eq_hq",
    )(x_index, in_hbm(q_t), in_hbm(e_t), in_hbm(h_t))


def products(t, x_ref, slabs):
    out = []
    for pair in range(0, slabs, 2):
        two = [x_ref[1024 * j : 1024 * (j + 1), :] for j in range(pair, min(pair + 2, slabs))]
        p = fold3(jnp.dot(t, jnp.concatenate(two, axis=1), preferred_element_type=F32))
        out += [p[:, 128 * s : 128 * (s + 1)] for s in range(len(two))]
    return out


def column_kernel(z_ref, *refs):
    messages, xs, (out_ref, t_ref, m_ref, x_ref, sems) = refs[:4], refs[4:11], refs[11:]
    loads = load_all(
        [(m, m_ref.at[i]) for i, m in enumerate(messages)]
        + [(v, x_ref.at[pl.ds(1024 * i, 1024), :]) for i, v in enumerate(xs)],
        sems,
    )
    for load in loads[:4]:
        load.wait()
    m = sum(m_ref[i].astype(F32) for i in range(4))
    t = split3(m[0:32] + m[32:64])
    t_ref[...] = t
    for z in range(8):
        out_ref[z] = m[64:96, 128 * z : 128 * (z + 1)]
    for load in loads[4:]:
        load.wait()
    for j, p in enumerate(products(t, x_ref, 7)):
        out_ref[z_ref[j]] += p


def column(z_index, messages, slabs):
    return pl.pallas_call(
        column_kernel,
        in_specs=[SMEM] + [ANY] * 11,
        out_specs=[VMEM] * 2,
        out_shape=[
            jax.ShapeDtypeStruct((8, 32, 128), F32),
            jax.ShapeDtypeStruct((96, 1024), BF16),
        ],
        scratch_shapes=[
            pltpu.VMEM((4, 96, 1024), BF16),
            pltpu.VMEM((7 * 1024, 128), BF16),
            pltpu.SemaphoreType.DMA((11,)),
        ],
        compiler_params=vmem(8),
        name="p_column",
    )(z_index, *messages, *slabs)


def column_rest_kernel(z_ref, part_ref, t_ref, *refs):
    slabs, (out_ref, x_ref, sems) = refs[:1], refs[1:]
    copies = [(v, x_ref.at[pl.ds(1024 * i, 1024), :]) for i, v in enumerate(slabs)]
    loads = load_all(copies, sems)
    out_ref[...] = part_ref[...]
    for load in loads:
        load.wait()
    for j, p in enumerate(products(t_ref[...], x_ref, 1)):
        out_ref[z_ref[7 + j]] += p


def column_rest(z_index, part, t, slabs):
    return pl.pallas_call(
        column_rest_kernel,
        in_specs=[SMEM] + [VMEM] * 2 + [ANY],
        out_specs=VMEM,
        out_shape=jax.ShapeDtypeStruct((8, 32, 128), F32),
        scratch_shapes=[pltpu.VMEM((1024, 128), BF16), pltpu.SemaphoreType.DMA((1,))],
        compiler_params=vmem(6),
        name="p_column_rest",
    )(z_index, part, t, *slabs)


def add_spread_kernel(scale, in_ref, out_ref):
    s = jnp.sum(in_ref[...], axis=0) * scale
    out_ref[...] = jnp.broadcast_to(s[None], out_ref.shape)


def add_spread(v, copies, scale):
    return pl.pallas_call(
        functools.partial(add_spread_kernel, scale),
        in_specs=[VMEM],
        out_specs=VMEM,
        out_shape=jax.ShapeDtypeStruct((copies, *v.shape[1:]), F32),
        compiler_params=vmem(4),
        name="add_spread",
    )(v)


def pack_kernel(*refs):
    parts, (out, sems) = refs[:-2], refs[-2:]
    copies = [(v, out.at[pl.ds(1024 * i, 1024), :]) for i, v in enumerate(parts)]
    for copy in load_all(copies, sems):
        copy.wait()


def pack(arrays):
    return pl.pallas_call(
        pack_kernel,
        in_specs=[ANY] * len(arrays),
        out_specs=HBM,
        out_shape=pltpu.HBM((1024 * len(arrays), 128), BF16),
        scratch_shapes=[pltpu.SemaphoreType.DMA((len(arrays),))],
        compiler_params=vmem(4),
        name="pack",
    )(*arrays)


def slab_copies(at_ref, first, e_hbm, x_hbm, e_ref, x_ref):
    slabs = [(r, i) for r in x_hbm for i in range(r.shape[0] // 1024)]
    pairs = []
    for place, (r, i) in enumerate(slabs):
        cols = pl.ds(pl.multiple_of(at_ref[first + place] * 128, 128), 128)
        pairs.append((r.at[pl.ds(1024 * i, 1024), :], x_ref.at[place]))
        pairs.append((e_hbm.at[:, cols], e_ref.at[place]))
    return pairs


def correct_pair(pair, loads, h_ref, e_ref, x_ref, out_ref):
    for load in loads[4 * pair : 4 * pair + 4]:
        load.wait()
    x = jnp.concatenate([x_ref[2 * pair], x_ref[2 * pair + 1]], axis=1)
    grad = jnp.dot(h_ref[...], x, preferred_element_type=F32)
    for s in range(2):
        place = 2 * pair + s
        both = e_ref[place].astype(F32) + grad[:, 128 * s : 128 * (s + 1)]
        out_ref[place] = both.astype(BF16)


def correct_kernel(at_ref, h_hbm, e_hbm, *refs):
    x_hbm, (out_ref, h_ref, e_ref, x_ref, sems) = refs[:-5], refs[-5:]
    copies = slab_copies(at_ref, 0, e_hbm, x_hbm, e_ref, x_ref)
    loads = load_all([(h_hbm, h_ref)] + copies, sems)
    loads[0].wait()
    for pair in range(at_ref.shape[0] // 2):
        correct_pair(pair, loads[1:], h_ref, e_ref, x_ref, out_ref)


def correct_scratch(n):
    return [
        pltpu.VMEM((448, 1024), BF16),
        pltpu.VMEM((n, 448, 128), BF16),
        pltpu.VMEM((n, 1024, 128), BF16),
        pltpu.SemaphoreType.DMA((1 + 2 * n,)),
    ]


def correct(places, h_t, e_t, arrays):
    n = places.shape[0]
    return pl.pallas_call(
        correct_kernel,
        in_specs=[SMEM] + [HBM] * (2 + len(arrays)),
        out_specs=VMEM,
        out_shape=pltpu.VMEM((n, 448, 128), BF16),
        scratch_shapes=correct_scratch(n),
        compiler_params=vmem(20),
        name="corrected",
    )(places, *[in_hbm(v) for v in [h_t, e_t, *arrays]])


def finish_kernel(kept_count, at_ref, p_ref, *refs):
    kept_refs, (h_hbm, e_hbm), refs = (
        refs[:kept_count],
        refs[kept_count : kept_count + 2],
        refs[kept_count + 2 :],
    )
    x_hbm, (w_ref, out_hbm, h_ref, e_ref, x_ref, sems, out_ref, out_sem) = refs[:-8], refs[-8:]
    rest = len(x_hbm)
    copies = slab_copies(at_ref, 32 - rest, e_hbm, x_hbm, e_ref, x_ref)
    loads = load_all([(h_hbm, h_ref)] + copies, sems)
    slabs = [(r, i) for r in [*kept_refs, out_ref] for i in range(r.shape[0])]

    def project_pair(pair):
        two = (2 * pair, 2 * pair + 1)
        p = jnp.concatenate([p_ref[at_ref[i]] for i in two], axis=1)
        c = jnp.concatenate([slabs[i][0][slabs[i][1]] for i in two], axis=1)
        return lax.dot_general(split3(p), c, NT, preferred_element_type=F32)

    total = sum(project_pair(pair) for pair in range(16 - rest // 2))
    loads[0].wait()
    for pair in range(rest // 2):
        correct_pair(pair, loads[1:], h_ref, e_ref, x_ref, out_ref)
    store = pltpu.make_async_copy(out_ref, out_hbm, out_sem)
    store.start()
    total = total + sum(project_pair(pair) for pair in range(16 - rest // 2, 16))
    w_ref[...] = fold3(total)
    store.wait()


def finish(places, p_blocks, kept, h_t, e_t, rest):
    n = len(rest)
    return pl.pallas_call(
        functools.partial(finish_kernel, len(kept)),
        in_specs=[SMEM] + [VMEM] * (1 + len(kept)) + [HBM] * (2 + n),
        out_specs=[VMEM, HBM],
        out_shape=[jax.ShapeDtypeStruct((32, 448), F32), pltpu.HBM((n, 448, 128), BF16)],
        scratch_shapes=correct_scratch(n)
        + [pltpu.VMEM((n, 448, 128), BF16), pltpu.SemaphoreType.DMA],
        compiler_params=vmem(14),
        name="c_p",
    )(places, p_blocks, *[in_vmem(v) for v in kept], *[in_hbm(v) for v in [h_t, e_t, *rest]])


def load_pieces(kept_refs, hbm, buffer, sem):
    load = pltpu.make_async_copy(hbm, buffer, sem)
    load.start()
    return [(r, i) for r in [*kept_refs, buffer] for i in range(r.shape[0])], load


def factor_kernel(p_ref, inv_ref, p_out_ref, low_ref):
    p = jnp.concatenate([p_ref[i] for i in range(32)], axis=1)
    gram = lax.dot_general(
        p, p, NT, precision=lax.Precision.HIGHEST, preferred_element_type=F32
    )
    row = lax.broadcasted_iota(jnp.int32, (32, 128), 0)
    col = lax.broadcasted_iota(jnp.int32, (32, 128), 1)
    work = jnp.concatenate([gram, jnp.zeros((32, 96), F32)], axis=1)
    work = jnp.where(col == row + 32, 1.0, work)
    scale = jnp.zeros((32, 1), F32)
    for j in range(32):
        pivot = work[j : j + 1, j : j + 1]
        below = jnp.where(row[:, :1] > j, work[:, j : j + 1], 0.0)
        scale = jnp.where(row[:, :1] == j, pivot, scale)
        work = work - below * (work[j : j + 1, :] / pivot)
    inverse = work[:, 32:64] / jnp.sqrt(scale)
    inv_ref[...] = inverse
    out = jnp.dot(inverse, p, precision=lax.Precision.HIGHEST, preferred_element_type=F32)
    p_out_ref[...] = out
    low_ref[...] = out.astype(BF16)


def factor(p_blocks):
    return pl.pallas_call(
        factor_kernel,
        in_specs=[VMEM],
        out_specs=[VMEM] * 3,
        out_shape=[
            jax.ShapeDtypeStruct((32, 32), F32),
            jax.ShapeDtypeStruct((32, 4096), F32),
            jax.ShapeDtypeStruct((32, 4096), BF16),
        ],
        compiler_params=vmem(8),
        name="factor",
    )(p_blocks)


def final_kernel(at_ref, inv_ref, a_ref, b_ref, c_ref, d_ref, low_ref, *refs):
    kept_refs, (c_hbm, q_ref, out_hbm, buffer, stage, sem, out_sems) = refs[:-7], refs[-7:]
    slabs, load = load_pieces(kept_refs, c_hbm, buffer, sem)
    w = (a_ref[...] + b_ref[...] + c_ref[...] + d_ref[...]) * 0.25
    q = jnp.dot(inv_ref[...], w, precision=lax.Precision.HIGHEST, preferred_element_type=F32)
    q_ref[...] = q
    rows = q.T.astype(BF16)
    stores = []
    for pair in range(16):
        if 2 * pair == 32 - buffer.shape[0]:
            load.wait()
        places = [pl.ds(pl.multiple_of(at_ref[2 * pair + s] * 128, 128), 128) for s in range(2)]
        p = jnp.concatenate([low_ref[:, place] for place in places], axis=1)
        approx = jnp.dot(rows, p, preferred_element_type=F32)
        for s, place in enumerate(places):
            i = 2 * pair + s
            kept = slabs[i][0][slabs[i][1]].astype(F32)
            stage[i] = (kept - approx[:, 128 * s : 128 * (s + 1)]).astype(BF16)
            store = pltpu.make_async_copy(stage.at[i], out_hbm.at[:, place], out_sems.at[i])
            store.start()
            stores.append(store)
    for store in stores:
        store.wait()


def final(places, inverse, parts, p_low, kept, piece):
    return pl.pallas_call(
        final_kernel,
        in_specs=[SMEM] + [VMEM] * (6 + len(kept)) + [HBM],
        out_specs=[VMEM, HBM],
        out_shape=[
            jax.ShapeDtypeStruct((32, 448), F32),
            jax.ShapeDtypeStruct((448, 4096), BF16),
        ],
        scratch_shapes=[
            pltpu.VMEM(piece.shape, BF16),
            pltpu.VMEM((32, 448, 128), BF16),
            pltpu.SemaphoreType.DMA,
            pltpu.SemaphoreType.DMA((32,)),
        ],
        compiler_params=vmem(14),
        name="new_error",
    )(places, inverse, *parts, p_low, *[in_vmem(v) for v in kept], in_hbm(piece))


def swap(v, axis="hidden", groups=None):
    return lax.all_to_all(v, axis, 0, 0, axis_index_groups=groups)


def replicas(v):
    return [v] + [
        lax.ppermute(v, "replica", [(i, (i + s) % 4) for i in range(4)]) for s in (1, 3, 2)
    ]


def move(v, dx, dz):
    pairs = [(h, (h // 8 + dx) % 4 * 8 + (h % 8 + dz) % 8) for h in range(32)]
    return lax.ppermute(v, "hidden", pairs)


def together(*values):
    return lax.optimization_barrier(values)


def shards(activations, hidden_grad, error_buffer, q_previous):
    x = activations[0]
    me = lax.axis_index("hidden")
    x_index, z_index = me // 8, me % 8
    z_order = jnp.stack([(z_index + rz) % 8 for rz in SOURCE_Z]).astype(jnp.int32)

    def places(rx):
        return (x_index + rx) % 4 * 8 + z_order

    e_t, h_t = error_buffer[0, 0].T, hidden_grad[0].T
    mine, *others = first(x_index.astype(jnp.int32)[None], q_previous[0].T, e_t, h_t)
    p1, m1, f0 = move(x, 0, 1), move(x, 0, -1), move(x, 2, 0)
    g1, g2, g3 = [move(m, dx, 0) for m, dx in zip(others, (1, 2, -1))]
    p1, m1, mine = together(p1, m1, mine)
    p2, m2 = move(p1, 0, 1), move(m1, 0, -1)
    p2, m2, f0 = together(p2, m2, f0)
    p3, m3 = move(p2, 0, 1), move(m2, 0, -1)
    fp1, fm1 = move(f0, 0, 1), move(f0, 0, -1)
    bundle = pack([x, p1, m1, p2, m2, p3, m3])
    p3, fp1, fm1 = together(p3, fp1, fm1)
    end = move(p3, 0, 1)
    bundle, g1, g2, g3 = together(bundle, g1, g2, g3)
    near = [move(bundle, 1, 0), move(bundle, -1, 0)]
    near_end = [move(end, 1, 0), move(end, -1, 0)]
    part, t = column(z_order, [mine, g1, g2, g3], [x, p1, m1, p2, m2, p3, m3])
    column_groups = [[8 * i + z for z in range(8)] for i in range(4)]
    p_parts = swap(column_rest(z_order, part, t, [end]), groups=column_groups)
    kept_own = correct(places(0), h_t, e_t, [bundle, end])
    fp2, fm2 = move(fp1, 0, 1), move(fm1, 0, -1)
    fp2, fm2, kept_own = together(fp2, fm2, kept_own)
    fp3, fm3, f_end = move(fp2, 0, 1), move(fm2, 0, -1), move(fm2, 0, -2)
    p_parts, kept_own = together(add_spread(p_parts, 4, 1.0), kept_own)
    p_parts = add_spread(swap(p_parts, "replica"), 32, 0.25)
    p_parts, fp3, fm3, f_end = together(p_parts, fp3, fm3, f_end)
    far = [f0, fp1, fm1, fp2, fm2, fp3, fm3, f_end]
    p_blocks = swap(p_parts)
    at_near = jnp.concatenate([places(-1)[:7], places(1)[:7]])
    at_rest = jnp.concatenate([places(-1)[7:], places(1)[7:], places(2)])
    at = jnp.concatenate([places(0), at_near, at_rest])
    kept = [kept_own, correct(at_near, h_t, e_t, near)]
    w_part, piece = finish(at, p_blocks, kept, h_t, e_t, [*near_end, *far])
    parts = replicas(w_part)
    inverse, p_factor, p_low = factor(p_blocks)
    q_factor, new_error = final(at, inverse, parts, p_low, kept, piece)
    return (p_factor.T[None], q_factor.T[None], new_error.T[None, None])


def solution(mesh):
    in_specs = (
        P("expert", "replica", "hidden"),
        P("expert", "replica", "hidden"),
        P("expert", "replica", None, "hidden"),
        P("expert", "hidden", None),
    )
    out_specs = (
        P("expert", None, None),
        P("expert", "hidden", None),
        P("expert", "replica", None, "hidden"),
    )
    return jax.shard_map(shards, mesh=mesh, in_specs=in_specs, out_specs=out_specs, check_vma=False)
```

```python
import functools

import jax
import jax.numpy as jnp
import numpy as np
from jax import lax
from jax.experimental import pallas as pl
from jax.experimental.pallas import tpu as pltpu
from jax.sharding import PartitionSpec as P

F32 = jnp.float32
BF16 = jnp.bfloat16
VMEM = pl.BlockSpec(memory_space=pltpu.VMEM)
SMEM = pl.BlockSpec(memory_space=pltpu.SMEM)
HBM = pl.BlockSpec(memory_space=pltpu.HBM)
ANY = pl.BlockSpec(memory_space=pl.ANY)


def vmem(mib):
    return pltpu.CompilerParams(vmem_limit_bytes=mib * 1024 * 1024)

NT = (((1,), (1,)), ((), ()))
TN = (((0,), (0,)), ((), ()))
SOURCE_Z = (0, -1, 1, -2, 2, -3, 3, 4)


def in_hbm(v):
    return pltpu.with_memory_space_constraint(v, pltpu.HBM)


def in_vmem(v):
    return pltpu.with_memory_space_constraint(v, pltpu.VMEM)


def load_all(pairs, sems):
    copies = [pltpu.make_async_copy(a, b, sems.at[i]) for i, (a, b) in enumerate(pairs)]
    for copy in copies:
        copy.start()
    return copies


def split3(v):
    a = v.astype(BF16)
    r = v - a.astype(F32)
    b = r.astype(BF16)
    c = (r - b.astype(F32)).astype(BF16)
    return jnp.concatenate([a, b, c], axis=0)


def fold3(v):
    n = v.shape[0] // 3
    return v[:n] + v[n : 2 * n] + v[2 * n :]


def first_kernel(x_ref, q_hbm, e_hbm, h_hbm, *refs):
    outs, (q_ref, e_ref, h_ref, sems) = refs[:4], refs[4:]
    columns = [pl.ds(pl.multiple_of((x_ref[0] + s) % 4 * 1024, 1024), 1024) for s in range(4)]
    loads = load_all(
        [(q_hbm, q_ref), (h_hbm, h_ref)]
        + [(e_hbm.at[:, columns[s]], e_ref.at[s]) for s in (1, 3, 2, 0)],
        sems,
    )
    loads[0].wait()
    q = q_ref[...].astype(BF16)
    loads[1].wait()
    t = jnp.dot(q, h_ref[...], preferred_element_type=F32)
    high = t.astype(BF16)
    low = (t - high.astype(F32)).astype(BF16)
    for load, s in zip(loads[2:], (1, 3, 2, 0)):
        load.wait()
        eq = jnp.dot(q, e_ref[s], preferred_element_type=F32)
        outs[s][0:32, :] = high
        outs[s][32:64, :] = low
        outs[s][64:96, :] = eq.astype(BF16)


def first(x_index, q_t, e_t, h_t):
    return pl.pallas_call(
        first_kernel,
        in_specs=[SMEM] + [HBM] * 3,
        out_specs=[VMEM] * 4,
        out_shape=[jax.ShapeDtypeStruct((96, 1024), BF16)] * 4,
        scratch_shapes=[
            pltpu.VMEM((32, 448), F32),
            pltpu.VMEM((4, 448, 1024), BF16),
            pltpu.VMEM((448, 1024), BF16),
            pltpu.SemaphoreType.DMA((6,)),
        ],
        compiler_params=vmem(12),
        name="eq_hq",
    )(x_index, in_hbm(q_t), in_hbm(e_t), in_hbm(h_t))


def products(t, x_ref, slabs):
    out = []
    for pair in range(0, slabs, 2):
        two = [x_ref[1024 * j : 1024 * (j + 1), :] for j in range(pair, min(pair + 2, slabs))]
        p = fold3(jnp.dot(t, jnp.concatenate(two, axis=1), preferred_element_type=F32))
        out += [p[:, 128 * s : 128 * (s + 1)] for s in range(len(two))]
    return out


def column_kernel(z_ref, *refs):
    messages, xs, (out_ref, t_ref, m_ref, x_ref, sems) = refs[:4], refs[4:11], refs[11:]
    loads = load_all(
        [(m, m_ref.at[i]) for i, m in enumerate(messages)]
        + [(v, x_ref.at[pl.ds(1024 * i, 1024), :]) for i, v in enumerate(xs)],
        sems,
    )
    for load in loads[:4]:
        load.wait()
    m = sum(m_ref[i].astype(F32) for i in range(4))
    t = split3(m[0:32] + m[32:64])
    t_ref[...] = t
    for z in range(8):
        out_ref[z] = m[64:96, 128 * z : 128 * (z + 1)]
    for load in loads[4:]:
        load.wait()
    for j, p in enumerate(products(t, x_ref, 7)):
        out_ref[z_ref[j]] += p


def column(z_index, messages, slabs):
    return pl.pallas_call(
        column_kernel,
        in_specs=[SMEM] + [ANY] * 11,
        out_specs=[VMEM] * 2,
        out_shape=[
            jax.ShapeDtypeStruct((8, 32, 128), F32),
            jax.ShapeDtypeStruct((96, 1024), BF16),
        ],
        scratch_shapes=[
            pltpu.VMEM((4, 96, 1024), BF16),
            pltpu.VMEM((7 * 1024, 128), BF16),
            pltpu.SemaphoreType.DMA((11,)),
        ],
        compiler_params=vmem(8),
        name="p_column",
    )(z_index, *messages, *slabs)


def column_rest_kernel(z_ref, part_ref, t_ref, *refs):
    slabs, (out_ref, x_ref, sems) = refs[:1], refs[1:]
    copies = [(v, x_ref.at[pl.ds(1024 * i, 1024), :]) for i, v in enumerate(slabs)]
    loads = load_all(copies, sems)
    out_ref[...] = part_ref[...]
    for load in loads:
        load.wait()
    for j, p in enumerate(products(t_ref[...], x_ref, 1)):
        out_ref[z_ref[7 + j]] += p


def column_rest(z_index, part, t, slabs):
    return pl.pallas_call(
        column_rest_kernel,
        in_specs=[SMEM] + [VMEM] * 2 + [ANY],
        out_specs=VMEM,
        out_shape=jax.ShapeDtypeStruct((8, 32, 128), F32),
        scratch_shapes=[pltpu.VMEM((1024, 128), BF16), pltpu.SemaphoreType.DMA((1,))],
        compiler_params=vmem(6),
        name="p_column_rest",
    )(z_index, part, t, *slabs)


def add_spread_kernel(scale, in_ref, out_ref):
    s = jnp.sum(in_ref[...], axis=0) * scale
    out_ref[...] = jnp.broadcast_to(s[None], out_ref.shape)


def add_spread(v, copies, scale):
    return pl.pallas_call(
        functools.partial(add_spread_kernel, scale),
        in_specs=[VMEM],
        out_specs=VMEM,
        out_shape=jax.ShapeDtypeStruct((copies, *v.shape[1:]), F32),
        compiler_params=vmem(4),
        name="add_spread",
    )(v)


def pack_kernel(*refs):
    parts, (out, sems) = refs[:-2], refs[-2:]
    copies = [(v, out.at[pl.ds(1024 * i, 1024), :]) for i, v in enumerate(parts)]
    for copy in load_all(copies, sems):
        copy.wait()


def pack(arrays):
    return pl.pallas_call(
        pack_kernel,
        in_specs=[ANY] * len(arrays),
        out_specs=HBM,
        out_shape=pltpu.HBM((1024 * len(arrays), 128), BF16),
        scratch_shapes=[pltpu.SemaphoreType.DMA((len(arrays),))],
        compiler_params=vmem(4),
        name="pack",
    )(*arrays)


def slab_copies(at_ref, first, e_hbm, x_hbm, parts_of, e_ref, x_ref):
    slabs = [(r, first_of + i) for r, (first_of, n) in zip(x_hbm, parts_of) for i in range(n)]
    pairs = []
    for place, (r, i) in enumerate(slabs):
        cols = pl.ds(pl.multiple_of(at_ref[first + place] * 128, 128), 128)
        pairs.append((r.at[pl.ds(1024 * i, 1024), :], x_ref.at[place]))
        pairs.append((e_hbm.at[:, cols], e_ref.at[place]))
    return pairs


def correct_pair(pair, loads, h_ref, e_ref, x_ref, out_ref):
    for load in loads[4 * pair : 4 * pair + 4]:
        load.wait()
    x = jnp.concatenate([x_ref[2 * pair], x_ref[2 * pair + 1]], axis=1)
    grad = jnp.dot(h_ref[...], x, preferred_element_type=F32)
    for s in range(2):
        place = 2 * pair + s
        both = e_ref[place].astype(F32) + grad[:, 128 * s : 128 * (s + 1)]
        out_ref[place] = both.astype(BF16)


def correct_kernel(parts_of, at_ref, h_hbm, e_hbm, *refs):
    x_hbm, (out_ref, h_ref, e_ref, x_ref, sems) = refs[:-5], refs[-5:]
    copies = slab_copies(at_ref, 0, e_hbm, x_hbm, parts_of, e_ref, x_ref)
    loads = load_all([(h_hbm, h_ref)] + copies, sems)
    loads[0].wait()
    for pair in range(at_ref.shape[0] // 2):
        correct_pair(pair, loads[1:], h_ref, e_ref, x_ref, out_ref)


def correct_scratch(n):
    return [
        pltpu.VMEM((448, 1024), BF16),
        pltpu.VMEM((n, 448, 128), BF16),
        pltpu.VMEM((n, 1024, 128), BF16),
        pltpu.SemaphoreType.DMA((1 + 2 * n,)),
    ]


def correct(places, h_t, e_t, arrays, parts_of):
    n = places.shape[0]
    return pl.pallas_call(
        functools.partial(correct_kernel, parts_of),
        in_specs=[SMEM] + [HBM] * (2 + len(arrays)),
        out_specs=VMEM,
        out_shape=pltpu.VMEM((n, 448, 128), BF16),
        scratch_shapes=correct_scratch(n),
        compiler_params=vmem(20),
        name="corrected",
    )(places, *[in_hbm(v) for v in [h_t, e_t, *arrays]])


def finish_kernel(kept_count, at_ref, p_ref, *refs):
    kept_refs, (h_hbm, e_hbm), refs = (
        refs[:kept_count],
        refs[kept_count : kept_count + 2],
        refs[kept_count + 2 :],
    )
    x_hbm, (w_ref, out_hbm, h_ref, e_ref, x_ref, sems, out_ref, out_sem) = refs[:-8], refs[-8:]
    rest = len(x_hbm)
    copies = slab_copies(at_ref, 32 - rest, e_hbm, x_hbm, [(0, 1)] * rest, e_ref, x_ref)
    loads = load_all([(h_hbm, h_ref)] + copies, sems)
    slabs = [(r, i) for r in [*kept_refs, out_ref] for i in range(r.shape[0])]

    def project_pair(pair):
        two = (2 * pair, 2 * pair + 1)
        p = jnp.concatenate([p_ref[at_ref[i]] for i in two], axis=1)
        c = jnp.concatenate([slabs[i][0][slabs[i][1]] for i in two], axis=1)
        return lax.dot_general(split3(p), c, NT, preferred_element_type=F32)

    total = sum(project_pair(pair) for pair in range(16 - rest // 2))
    loads[0].wait()
    for pair in range(rest // 2):
        correct_pair(pair, loads[1:], h_ref, e_ref, x_ref, out_ref)
    store = pltpu.make_async_copy(out_ref, out_hbm, out_sem)
    store.start()
    total = total + sum(project_pair(pair) for pair in range(16 - rest // 2, 16))
    w_ref[...] = fold3(total)
    store.wait()


def finish(places, p_blocks, kept, h_t, e_t, rest):
    n = len(rest)
    return pl.pallas_call(
        functools.partial(finish_kernel, len(kept)),
        in_specs=[SMEM] + [VMEM] * (1 + len(kept)) + [HBM] * (2 + n),
        out_specs=[VMEM, HBM],
        out_shape=[jax.ShapeDtypeStruct((32, 448), F32), pltpu.HBM((n, 448, 128), BF16)],
        scratch_shapes=correct_scratch(n)
        + [pltpu.VMEM((n, 448, 128), BF16), pltpu.SemaphoreType.DMA],
        compiler_params=vmem(14),
        name="c_p",
    )(places, p_blocks, *[in_vmem(v) for v in kept], *[in_hbm(v) for v in [h_t, e_t, *rest]])


def load_pieces(kept_refs, hbm, buffer, sem):
    load = pltpu.make_async_copy(hbm, buffer, sem)
    load.start()
    return [(r, i) for r in [*kept_refs, buffer] for i in range(r.shape[0])], load


def factor_kernel(p_ref, inv_ref, p_out_ref, low_ref):
    p = split3(jnp.concatenate([p_ref[i] for i in range(32)], axis=1))
    gram = fold3(lax.dot_general(p, p, NT, preferred_element_type=F32))
    gram = gram[:, 0:32] + gram[:, 32:64] + gram[:, 64:96]
    row = lax.broadcasted_iota(jnp.int32, (32, 128), 0)
    col = lax.broadcasted_iota(jnp.int32, (32, 128), 1)
    work = jnp.concatenate([gram, jnp.zeros((32, 96), F32)], axis=1)
    work = jnp.where(col == row + 32, 1.0, work)
    scale = jnp.zeros((32, 1), F32)
    for j in range(32):
        pivot = work[j : j + 1, j : j + 1]
        below = jnp.where(row[:, :1] > j, work[:, j : j + 1], 0.0)
        scale = jnp.where(row[:, :1] == j, pivot, scale)
        work = work - below * (work[j : j + 1, :] / pivot)
    inverse = work[:, 32:64] / jnp.sqrt(scale)
    inv_ref[...] = inverse
    terms = split3(inverse)
    terms = jnp.concatenate([terms, terms, terms], axis=1)
    out = fold3(jnp.dot(terms, p, preferred_element_type=F32))
    p_out_ref[...] = out
    low_ref[...] = out.astype(BF16)


def factor(p_blocks):
    return pl.pallas_call(
        factor_kernel,
        in_specs=[VMEM],
        out_specs=[VMEM] * 3,
        out_shape=[
            jax.ShapeDtypeStruct((32, 32), F32),
            jax.ShapeDtypeStruct((32, 4096), F32),
            jax.ShapeDtypeStruct((32, 4096), BF16),
        ],
        compiler_params=vmem(8),
        name="factor",
    )(p_blocks)


def final_kernel(at_ref, inv_ref, a_ref, b_ref, c_ref, d_ref, low_ref, *refs):
    kept_refs, (c_hbm, q_ref, out_hbm, buffer, stage, sem, out_sems) = refs[:-7], refs[-7:]
    slabs, load = load_pieces(kept_refs, c_hbm, buffer, sem)
    w = (a_ref[...] + b_ref[...] + c_ref[...] + d_ref[...]) * 0.25
    q = jnp.dot(inv_ref[...], w, precision=lax.Precision.HIGHEST, preferred_element_type=F32)
    q_ref[...] = q
    rows = q.T.astype(BF16)
    stores = []
    for pair in range(16):
        if 2 * pair == 32 - buffer.shape[0]:
            load.wait()
        places = [pl.ds(pl.multiple_of(at_ref[2 * pair + s] * 128, 128), 128) for s in range(2)]
        p = jnp.concatenate([low_ref[:, place] for place in places], axis=1)
        approx = jnp.dot(rows, p, preferred_element_type=F32)
        for s, place in enumerate(places):
            i = 2 * pair + s
            kept = slabs[i][0][slabs[i][1]].astype(F32)
            stage[i] = (kept - approx[:, 128 * s : 128 * (s + 1)]).astype(BF16)
            store = pltpu.make_async_copy(stage.at[i], out_hbm.at[:, place], out_sems.at[i])
            store.start()
            stores.append(store)
    for store in stores:
        store.wait()


def final(places, inverse, parts, p_low, kept, piece):
    return pl.pallas_call(
        final_kernel,
        in_specs=[SMEM] + [VMEM] * (6 + len(kept)) + [HBM],
        out_specs=[VMEM, HBM],
        out_shape=[
            jax.ShapeDtypeStruct((32, 448), F32),
            jax.ShapeDtypeStruct((448, 4096), BF16),
        ],
        scratch_shapes=[
            pltpu.VMEM(piece.shape, BF16),
            pltpu.VMEM((32, 448, 128), BF16),
            pltpu.SemaphoreType.DMA,
            pltpu.SemaphoreType.DMA((32,)),
        ],
        compiler_params=vmem(14),
        name="new_error",
    )(places, inverse, *parts, p_low, *[in_vmem(v) for v in kept], in_hbm(piece))


def swap(v, axis="hidden", groups=None):
    return lax.all_to_all(v, axis, 0, 0, axis_index_groups=groups)


def replicas(v):
    return [v] + [
        lax.ppermute(v, "replica", [(i, (i + s) % 4) for i in range(4)]) for s in (1, 3, 2)
    ]


def move(v, dx, dz):
    pairs = [(h, (h // 8 + dx) % 4 * 8 + (h % 8 + dz) % 8) for h in range(32)]
    return lax.ppermute(v, "hidden", pairs)


def together(*values):
    return lax.optimization_barrier(values)


def shards(activations, hidden_grad, error_buffer, q_previous):
    x = activations[0]
    me = lax.axis_index("hidden")
    x_index, z_index = me // 8, me % 8
    z_order = jnp.stack([(z_index + rz) % 8 for rz in SOURCE_Z]).astype(jnp.int32)

    def places(*columns):
        rx = np.concatenate([np.full(len(rz), r) for r, rz in columns]).astype(np.int32)
        rz = np.concatenate([rz for _, rz in columns]).astype(np.int32)
        return ((x_index + rx) % 4 * 8 + (z_index + rz) % 8).astype(jnp.int32)

    e_t, h_t = error_buffer[0, 0].T, hidden_grad[0].T
    mine, *others = first(x_index.astype(jnp.int32)[None], q_previous[0].T, e_t, h_t)
    p1, m1, f0 = move(x, 0, 1), move(x, 0, -1), move(x, 2, 0)
    g1, g2, g3 = [move(m, dx, 0) for m, dx in zip(others, (1, 2, -1))]
    p1, m1, mine = together(p1, m1, mine)
    p2, m2 = move(p1, 0, 1), move(m1, 0, -1)
    p2, m2, f0 = together(p2, m2, f0)
    p3, m3 = move(p2, 0, 1), move(m2, 0, -1)
    fp1, fm1 = move(f0, 0, 1), move(f0, 0, -1)
    bundle = pack([x, p1, m1, p2, m2, p3, m3])
    p3, fp1, fm1 = together(p3, fp1, fm1)
    end = move(p3, 0, 1)
    bundle, g1, g2, g3 = together(bundle, g1, g2, g3)
    near = [move(bundle, 1, 0), move(bundle, -1, 0)]
    near_end = [move(end, 1, 0), move(end, -1, 0)]
    part, t = column(z_order, [mine, g1, g2, g3], [x, p1, m1, p2, m2, p3, m3])
    column_groups = [[8 * i + z for z in range(8)] for i in range(4)]
    p_parts = swap(column_rest(z_order, part, t, [end]), groups=column_groups)
    own_early, own_late = (0, SOURCE_Z[:4]), (0, SOURCE_Z[4:])
    kept_own = correct(places(own_early), h_t, e_t, [bundle], [(0, 4)])
    fp2, fm2 = move(fp1, 0, 1), move(fm1, 0, -1)
    fp2, fm2, kept_own = together(fp2, fm2, kept_own)
    fp3, fm3, f_end = move(fp2, 0, 1), move(fm2, 0, -1), move(fm2, 0, -2)
    p_parts, kept_own = together(add_spread(p_parts, 4, 1.0), kept_own)
    p_parts = add_spread(swap(p_parts, "replica"), 32, 0.25)
    kept_late = correct(places(own_late), h_t, e_t, [bundle, end], [(4, 3), (0, 1)])
    p_parts, fp3, fm3, f_end, kept_late = together(p_parts, fp3, fm3, f_end, kept_late)
    far = [f0, fp1, fm1, fp2, fm2, fp3, fm3, f_end]
    p_blocks = swap(p_parts)
    middle = [(-1, SOURCE_Z[:7]), (1, SOURCE_Z[:7]), (2, SOURCE_Z[:4])]
    rest = [(-1, SOURCE_Z[7:]), (1, SOURCE_Z[7:]), (2, SOURCE_Z[4:])]
    at = places(own_early, own_late, *middle, *rest)
    parts_of = [(0, 7), (0, 7)] + [(0, 1)] * 4
    kept_middle = correct(places(*middle), h_t, e_t, [*near, *far[:4]], parts_of)
    kept = [kept_own, kept_late, kept_middle]
    w_part, piece = finish(at, p_blocks, kept, h_t, e_t, [*near_end, *far[4:]])
    parts = replicas(w_part)
    inverse, p_factor, p_low = factor(p_blocks)
    q_factor, new_error = final(at, inverse, parts, p_low, kept, piece)
    return (p_factor.T[None], q_factor.T[None], new_error.T[None, None])


def solution(mesh):
    in_specs = (
        P("expert", "replica", "hidden"),
        P("expert", "replica", "hidden"),
        P("expert", "replica", None, "hidden"),
        P("expert", "hidden", None),
    )
    out_specs = (
        P("expert", None, None),
        P("expert", "hidden", None),
        P("expert", "replica", None, "hidden"),
    )
    return jax.shard_map(shards, mesh=mesh, in_specs=in_specs, out_specs=out_specs, check_vma=False)
```

```python
import functools

import jax
import jax.numpy as jnp
import numpy as np
from jax import lax
from jax.experimental import pallas as pl
from jax.experimental.pallas import tpu as pltpu
from jax.sharding import PartitionSpec as P

F32 = jnp.float32
BF16 = jnp.bfloat16
VMEM = pl.BlockSpec(memory_space=pltpu.VMEM)
SMEM = pl.BlockSpec(memory_space=pltpu.SMEM)
HBM = pl.BlockSpec(memory_space=pltpu.HBM)
ANY = pl.BlockSpec(memory_space=pl.ANY)


def vmem(mib):
    return pltpu.CompilerParams(vmem_limit_bytes=mib * 1024 * 1024)

NT = (((1,), (1,)), ((), ()))
TN = (((0,), (0,)), ((), ()))
SOURCE_Z = (0, -1, 1, -2, 2, -3, 3, 4)


def in_hbm(v):
    return pltpu.with_memory_space_constraint(v, pltpu.HBM)


def in_vmem(v):
    return pltpu.with_memory_space_constraint(v, pltpu.VMEM)


def load_all(pairs, sems):
    copies = [pltpu.make_async_copy(a, b, sems.at[i]) for i, (a, b) in enumerate(pairs)]
    for copy in copies:
        copy.start()
    return copies


def split3(v):
    a = v.astype(BF16)
    r = v - a.astype(F32)
    b = r.astype(BF16)
    c = (r - b.astype(F32)).astype(BF16)
    return jnp.concatenate([a, b, c], axis=0)


def fold3(v):
    n = v.shape[0] // 3
    return v[:n] + v[n : 2 * n] + v[2 * n :]


def first_kernel(x_ref, q_hbm, e_hbm, h_hbm, *refs):
    outs, (q_ref, e_ref, h_ref, sems) = refs[:4], refs[4:]
    columns = [pl.ds(pl.multiple_of((x_ref[0] + s) % 4 * 1024, 1024), 1024) for s in range(4)]
    loads = load_all(
        [(q_hbm, q_ref), (h_hbm, h_ref)]
        + [(e_hbm.at[:, columns[s]], e_ref.at[s]) for s in (1, 3, 2, 0)],
        sems,
    )
    loads[0].wait()
    q = q_ref[...].astype(BF16)
    loads[1].wait()
    t = jnp.dot(q, h_ref[...], preferred_element_type=F32)
    high = t.astype(BF16)
    low = (t - high.astype(F32)).astype(BF16)
    for load, s in zip(loads[2:], (1, 3, 2, 0)):
        load.wait()
        eq = jnp.dot(q, e_ref[s], preferred_element_type=F32)
        outs[s][0:32, :] = high
        outs[s][32:64, :] = low
        outs[s][64:96, :] = eq.astype(BF16)


def first(x_index, q_t, e_t, h_t):
    return pl.pallas_call(
        first_kernel,
        in_specs=[SMEM] + [HBM] * 3,
        out_specs=[VMEM] * 4,
        out_shape=[jax.ShapeDtypeStruct((96, 1024), BF16)] * 4,
        scratch_shapes=[
            pltpu.VMEM((32, 448), F32),
            pltpu.VMEM((4, 448, 1024), BF16),
            pltpu.VMEM((448, 1024), BF16),
            pltpu.SemaphoreType.DMA((6,)),
        ],
        compiler_params=vmem(12),
        name="eq_hq",
    )(x_index, in_hbm(q_t), in_hbm(e_t), in_hbm(h_t))


def products(t, x_ref, slabs):
    out = []
    for pair in range(0, slabs, 2):
        two = [x_ref[1024 * j : 1024 * (j + 1), :] for j in range(pair, min(pair + 2, slabs))]
        p = fold3(jnp.dot(t, jnp.concatenate(two, axis=1), preferred_element_type=F32))
        out += [p[:, 128 * s : 128 * (s + 1)] for s in range(len(two))]
    return out


def column_kernel(z_ref, *refs):
    messages, xs, (out_ref, t_ref, m_ref, x_ref, sems) = refs[:4], refs[4:11], refs[11:]
    loads = load_all(
        [(m, m_ref.at[i]) for i, m in enumerate(messages)]
        + [(v, x_ref.at[pl.ds(1024 * i, 1024), :]) for i, v in enumerate(xs)],
        sems,
    )
    for load in loads[:4]:
        load.wait()
    m = sum(m_ref[i].astype(F32) for i in range(4))
    t = split3(m[0:32] + m[32:64])
    t_ref[...] = t
    for z in range(8):
        out_ref[z] = m[64:96, 128 * z : 128 * (z + 1)]
    for load in loads[4:]:
        load.wait()
    for j, p in enumerate(products(t, x_ref, 7)):
        out_ref[z_ref[j]] += p


def column(z_index, messages, slabs):
    return pl.pallas_call(
        column_kernel,
        in_specs=[SMEM] + [ANY] * 11,
        out_specs=[VMEM] * 2,
        out_shape=[
            jax.ShapeDtypeStruct((8, 32, 128), F32),
            jax.ShapeDtypeStruct((96, 1024), BF16),
        ],
        scratch_shapes=[
            pltpu.VMEM((4, 96, 1024), BF16),
            pltpu.VMEM((7 * 1024, 128), BF16),
            pltpu.SemaphoreType.DMA((11,)),
        ],
        compiler_params=vmem(8),
        name="p_column",
    )(z_index, *messages, *slabs)


def column_rest_kernel(z_ref, part_ref, t_ref, *refs):
    slabs, (out_ref, x_ref, sems) = refs[:1], refs[1:]
    copies = [(v, x_ref.at[pl.ds(1024 * i, 1024), :]) for i, v in enumerate(slabs)]
    loads = load_all(copies, sems)
    out_ref[...] = part_ref[...]
    for load in loads:
        load.wait()
    for j, p in enumerate(products(t_ref[...], x_ref, 1)):
        out_ref[z_ref[7 + j]] += p


def column_rest(z_index, part, t, slabs):
    return pl.pallas_call(
        column_rest_kernel,
        in_specs=[SMEM] + [VMEM] * 2 + [ANY],
        out_specs=VMEM,
        out_shape=jax.ShapeDtypeStruct((8, 32, 128), F32),
        scratch_shapes=[pltpu.VMEM((1024, 128), BF16), pltpu.SemaphoreType.DMA((1,))],
        compiler_params=vmem(6),
        name="p_column_rest",
    )(z_index, part, t, *slabs)


def add_spread_kernel(scale, in_ref, out_ref):
    s = jnp.sum(in_ref[...], axis=0) * scale
    out_ref[...] = jnp.broadcast_to(s[None], out_ref.shape)


def add_spread(v, copies, scale):
    return pl.pallas_call(
        functools.partial(add_spread_kernel, scale),
        in_specs=[VMEM],
        out_specs=VMEM,
        out_shape=jax.ShapeDtypeStruct((copies, *v.shape[1:]), F32),
        compiler_params=vmem(4),
        name="add_spread",
    )(v)


def pack_kernel(*refs):
    parts, (out, sems) = refs[:-2], refs[-2:]
    copies = [(v, out.at[pl.ds(1024 * i, 1024), :]) for i, v in enumerate(parts)]
    for copy in load_all(copies, sems):
        copy.wait()


def pack(arrays):
    return pl.pallas_call(
        pack_kernel,
        in_specs=[ANY] * len(arrays),
        out_specs=HBM,
        out_shape=pltpu.HBM((1024 * len(arrays), 128), BF16),
        scratch_shapes=[pltpu.SemaphoreType.DMA((len(arrays),))],
        compiler_params=vmem(4),
        name="pack",
    )(*arrays)


def slab_copies(at_ref, first, e_hbm, x_hbm, parts_of, e_ref, x_ref):
    slabs = [(r, first_of + i) for r, (first_of, n) in zip(x_hbm, parts_of) for i in range(n)]
    pairs = []
    for place, (r, i) in enumerate(slabs):
        cols = pl.ds(pl.multiple_of(at_ref[first + place] * 128, 128), 128)
        pairs.append((r.at[pl.ds(1024 * i, 1024), :], x_ref.at[place]))
        pairs.append((e_hbm.at[:, cols], e_ref.at[place]))
    return pairs


def correct_pair(pair, loads, h_ref, e_ref, x_ref, out_ref):
    for load in loads[4 * pair : 4 * pair + 4]:
        load.wait()
    x = jnp.concatenate([x_ref[2 * pair], x_ref[2 * pair + 1]], axis=1)
    grad = jnp.dot(h_ref[...], x, preferred_element_type=F32)
    for s in range(2):
        place = 2 * pair + s
        both = e_ref[place].astype(F32) + grad[:, 128 * s : 128 * (s + 1)]
        out_ref[place] = both.astype(BF16)


def correct_kernel(parts_of, at_ref, h_hbm, e_hbm, *refs):
    x_hbm, (out_ref, h_ref, e_ref, x_ref, sems) = refs[:-5], refs[-5:]
    copies = slab_copies(at_ref, 0, e_hbm, x_hbm, parts_of, e_ref, x_ref)
    loads = load_all([(h_hbm, h_ref)] + copies, sems)
    loads[0].wait()
    for pair in range(at_ref.shape[0] // 2):
        correct_pair(pair, loads[1:], h_ref, e_ref, x_ref, out_ref)


def correct_scratch(n):
    return [
        pltpu.VMEM((448, 1024), BF16),
        pltpu.VMEM((n, 448, 128), BF16),
        pltpu.VMEM((n, 1024, 128), BF16),
        pltpu.SemaphoreType.DMA((1 + 2 * n,)),
    ]


def correct(places, h_t, e_t, arrays, parts_of):
    n = places.shape[0]
    return pl.pallas_call(
        functools.partial(correct_kernel, parts_of),
        in_specs=[SMEM] + [HBM] * (2 + len(arrays)),
        out_specs=VMEM,
        out_shape=pltpu.VMEM((n, 448, 128), BF16),
        scratch_shapes=correct_scratch(n),
        compiler_params=vmem(20),
        name="corrected",
    )(places, *[in_hbm(v) for v in [h_t, e_t, *arrays]])


def finish_kernel(kept_count, at_ref, p_ref, *refs):
    kept_refs, (h_hbm, e_hbm), refs = (
        refs[:kept_count],
        refs[kept_count : kept_count + 2],
        refs[kept_count + 2 :],
    )
    x_hbm, (w_ref, out_hbm, h_ref, e_ref, x_ref, sems, out_ref, out_sem) = refs[:-8], refs[-8:]
    rest = len(x_hbm)
    copies = slab_copies(at_ref, 32 - rest, e_hbm, x_hbm, [(0, 1)] * rest, e_ref, x_ref)
    loads = load_all([(h_hbm, h_ref)] + copies, sems)
    slabs = [(r, i) for r in [*kept_refs, out_ref] for i in range(r.shape[0])]

    def project_pair(pair):
        two = (2 * pair, 2 * pair + 1)
        p = jnp.concatenate([p_ref[at_ref[i]] for i in two], axis=1)
        c = jnp.concatenate([slabs[i][0][slabs[i][1]] for i in two], axis=1)
        return lax.dot_general(split3(p), c, NT, preferred_element_type=F32)

    total = sum(project_pair(pair) for pair in range(16 - rest // 2))
    loads[0].wait()
    for pair in range(rest // 2):
        correct_pair(pair, loads[1:], h_ref, e_ref, x_ref, out_ref)
    store = pltpu.make_async_copy(out_ref, out_hbm, out_sem)
    store.start()
    total = total + sum(project_pair(pair) for pair in range(16 - rest // 2, 16))
    w_ref[...] = fold3(total)
    store.wait()


def finish(places, p_blocks, kept, h_t, e_t, rest):
    n = len(rest)
    return pl.pallas_call(
        functools.partial(finish_kernel, len(kept)),
        in_specs=[SMEM] + [VMEM] * (1 + len(kept)) + [HBM] * (2 + n),
        out_specs=[VMEM, HBM],
        out_shape=[jax.ShapeDtypeStruct((32, 448), F32), pltpu.HBM((n, 448, 128), BF16)],
        scratch_shapes=correct_scratch(n)
        + [pltpu.VMEM((n, 448, 128), BF16), pltpu.SemaphoreType.DMA],
        compiler_params=vmem(14),
        name="c_p",
    )(places, p_blocks, *[in_vmem(v) for v in kept], *[in_hbm(v) for v in [h_t, e_t, *rest]])


def load_pieces(kept_refs, hbm, buffer, sem):
    load = pltpu.make_async_copy(hbm, buffer, sem)
    load.start()
    return [(r, i) for r in [*kept_refs, buffer] for i in range(r.shape[0])], load


def factor_kernel(p_ref, inv_ref, p_out_ref, low_ref):
    p = split3(jnp.concatenate([p_ref[i] for i in range(32)], axis=1))
    gram = fold3(lax.dot_general(p, p, NT, preferred_element_type=F32))
    gram = gram[:, 0:32] + gram[:, 32:64] + gram[:, 64:96]
    row = lax.broadcasted_iota(jnp.int32, (32, 128), 0)
    col = lax.broadcasted_iota(jnp.int32, (32, 128), 1)
    work = jnp.concatenate([gram, jnp.zeros((32, 96), F32)], axis=1)
    work = jnp.where(col == row + 32, 1.0, work)
    scale = jnp.zeros((32, 128), F32)
    for start in range(0, 32, 8):
        block = range(start, start + 8)
        columns = {j: jnp.broadcast_to(work[:, j : j + 1], (32, 128)) for j in block}
        for j in block:
            pivot = columns[j][j : j + 1, :]
            scale = jnp.where(row == j, pivot, scale)
            below = jnp.where(row > j, columns[j], 0.0) * (1.0 / pivot)
            work = work - below * work[j : j + 1, :]
            for k in range(j + 1, start + 8):
                columns[k] = columns[k] - below * columns[k][j : j + 1, :]
    inverse = (work / jnp.sqrt(scale))[:, 32:64]
    inv_ref[...] = inverse
    terms = split3(inverse)
    terms = jnp.concatenate([terms, terms, terms], axis=1)
    out = fold3(jnp.dot(terms, p, preferred_element_type=F32))
    p_out_ref[...] = out
    low_ref[...] = out.astype(BF16)


def factor(p_blocks):
    return pl.pallas_call(
        factor_kernel,
        in_specs=[VMEM],
        out_specs=[VMEM] * 3,
        out_shape=[
            jax.ShapeDtypeStruct((32, 32), F32),
            jax.ShapeDtypeStruct((32, 4096), F32),
            jax.ShapeDtypeStruct((32, 4096), BF16),
        ],
        compiler_params=vmem(8),
        name="factor",
    )(p_blocks)


def final_kernel(at_ref, inv_ref, a_ref, b_ref, c_ref, d_ref, low_ref, *refs):
    kept_refs, (c_hbm, q_ref, out_hbm, buffer, stage, sem, out_sems) = refs[:-7], refs[-7:]
    slabs, load = load_pieces(kept_refs, c_hbm, buffer, sem)
    w = (a_ref[...] + b_ref[...] + c_ref[...] + d_ref[...]) * 0.25
    q = jnp.dot(inv_ref[...], w, precision=lax.Precision.HIGHEST, preferred_element_type=F32)
    q_ref[...] = q
    rows = q.T.astype(BF16)
    stores = []
    for pair in range(16):
        if 2 * pair == 32 - buffer.shape[0]:
            load.wait()
        places = [pl.ds(pl.multiple_of(at_ref[2 * pair + s] * 128, 128), 128) for s in range(2)]
        p = jnp.concatenate([low_ref[:, place] for place in places], axis=1)
        approx = jnp.dot(rows, p, preferred_element_type=F32)
        for s, place in enumerate(places):
            i = 2 * pair + s
            kept = slabs[i][0][slabs[i][1]].astype(F32)
            stage[i] = (kept - approx[:, 128 * s : 128 * (s + 1)]).astype(BF16)
            store = pltpu.make_async_copy(stage.at[i], out_hbm.at[:, place], out_sems.at[i])
            store.start()
            stores.append(store)
    for store in stores:
        store.wait()


def final(places, inverse, parts, p_low, kept, piece):
    return pl.pallas_call(
        final_kernel,
        in_specs=[SMEM] + [VMEM] * (6 + len(kept)) + [HBM],
        out_specs=[VMEM, HBM],
        out_shape=[
            jax.ShapeDtypeStruct((32, 448), F32),
            jax.ShapeDtypeStruct((448, 4096), BF16),
        ],
        scratch_shapes=[
            pltpu.VMEM(piece.shape, BF16),
            pltpu.VMEM((32, 448, 128), BF16),
            pltpu.SemaphoreType.DMA,
            pltpu.SemaphoreType.DMA((32,)),
        ],
        compiler_params=vmem(14),
        name="new_error",
    )(places, inverse, *parts, p_low, *[in_vmem(v) for v in kept], in_hbm(piece))


def swap(v, axis="hidden", groups=None):
    return lax.all_to_all(v, axis, 0, 0, axis_index_groups=groups)


def replicas(v):
    return [v] + [
        lax.ppermute(v, "replica", [(i, (i + s) % 4) for i in range(4)]) for s in (1, 3, 2)
    ]


def move(v, dx, dz):
    pairs = [(h, (h // 8 + dx) % 4 * 8 + (h % 8 + dz) % 8) for h in range(32)]
    return lax.ppermute(v, "hidden", pairs)


def together(*values):
    return lax.optimization_barrier(values)


def shards(activations, hidden_grad, error_buffer, q_previous):
    x = activations[0]
    me = lax.axis_index("hidden")
    x_index, z_index = me // 8, me % 8
    z_order = jnp.stack([(z_index + rz) % 8 for rz in SOURCE_Z]).astype(jnp.int32)

    def places(*columns):
        rx = np.concatenate([np.full(len(rz), r) for r, rz in columns]).astype(np.int32)
        rz = np.concatenate([rz for _, rz in columns]).astype(np.int32)
        return ((x_index + rx) % 4 * 8 + (z_index + rz) % 8).astype(jnp.int32)

    e_t, h_t = error_buffer[0, 0].T, hidden_grad[0].T
    mine, *others = first(x_index.astype(jnp.int32)[None], q_previous[0].T, e_t, h_t)
    p1, m1, f0 = move(x, 0, 1), move(x, 0, -1), move(x, 2, 0)
    g1, g2, g3 = [move(m, dx, 0) for m, dx in zip(others, (1, 2, -1))]
    p1, m1, mine = together(p1, m1, mine)
    p2, m2 = move(p1, 0, 1), move(m1, 0, -1)
    p2, m2, f0 = together(p2, m2, f0)
    p3, m3 = move(p2, 0, 1), move(m2, 0, -1)
    fp1, fm1 = move(f0, 0, 1), move(f0, 0, -1)
    bundle = pack([x, p1, m1, p2, m2, p3, m3])
    p3, fp1, fm1 = together(p3, fp1, fm1)
    end = move(p3, 0, 1)
    bundle, g1, g2, g3 = together(bundle, g1, g2, g3)
    near = [move(bundle, 1, 0), move(bundle, -1, 0)]
    near_end = [move(end, 1, 0), move(end, -1, 0)]
    part, t = column(z_order, [mine, g1, g2, g3], [x, p1, m1, p2, m2, p3, m3])
    column_groups = [[8 * i + z for z in range(8)] for i in range(4)]
    p_parts = swap(column_rest(z_order, part, t, [end]), groups=column_groups)
    own_early, own_late = (0, SOURCE_Z[:4]), (0, SOURCE_Z[4:])
    kept_own = correct(places(own_early), h_t, e_t, [bundle], [(0, 4)])
    fp2, fm2 = move(fp1, 0, 1), move(fm1, 0, -1)
    fp2, fm2, kept_own = together(fp2, fm2, kept_own)
    fp3, fm3, f_end = move(fp2, 0, 1), move(fm2, 0, -1), move(fm2, 0, -2)
    p_parts, kept_own = together(add_spread(p_parts, 4, 1.0), kept_own)
    p_parts = add_spread(swap(p_parts, "replica"), 32, 0.25)
    kept_late = correct(places(own_late), h_t, e_t, [bundle, end], [(4, 3), (0, 1)])
    p_parts, fp3, fm3, f_end, kept_late = together(p_parts, fp3, fm3, f_end, kept_late)
    far = [f0, fp1, fm1, fp2, fm2, fp3, fm3, f_end]
    p_blocks = swap(p_parts)
    middle = [(-1, SOURCE_Z[:7]), (1, SOURCE_Z[:7]), (2, SOURCE_Z[:4])]
    rest = [(-1, SOURCE_Z[7:]), (1, SOURCE_Z[7:]), (2, SOURCE_Z[4:])]
    at = places(own_early, own_late, *middle, *rest)
    parts_of = [(0, 7), (0, 7)] + [(0, 1)] * 4
    kept_middle = correct(places(*middle), h_t, e_t, [*near, *far[:4]], parts_of)
    kept = [kept_own, kept_late, kept_middle]
    w_part, piece = finish(at, p_blocks, kept, h_t, e_t, [*near_end, *far[4:]])
    parts = replicas(w_part)
    inverse, p_factor, p_low = factor(p_blocks)
    q_factor, new_error = final(at, inverse, parts, p_low, kept, piece)
    return (p_factor.T[None], q_factor.T[None], new_error.T[None, None])


def solution(mesh):
    in_specs = (
        P("expert", "replica", "hidden"),
        P("expert", "replica", "hidden"),
        P("expert", "replica", None, "hidden"),
        P("expert", "hidden", None),
    )
    out_specs = (
        P("expert", None, None),
        P("expert", "hidden", None),
        P("expert", "replica", None, "hidden"),
    )
    return jax.shard_map(shards, mesh=mesh, in_specs=in_specs, out_specs=out_specs, check_vma=False)
```

```python
import functools

import jax
import jax.numpy as jnp
import numpy as np
from jax import lax
from jax.experimental import pallas as pl
from jax.experimental.pallas import tpu as pltpu
from jax.sharding import PartitionSpec as P

F32 = jnp.float32
BF16 = jnp.bfloat16
VMEM = pl.BlockSpec(memory_space=pltpu.VMEM)
SMEM = pl.BlockSpec(memory_space=pltpu.SMEM)
HBM = pl.BlockSpec(memory_space=pltpu.HBM)
ANY = pl.BlockSpec(memory_space=pl.ANY)


def vmem(mib):
    return pltpu.CompilerParams(vmem_limit_bytes=mib * 1024 * 1024)

NT = (((1,), (1,)), ((), ()))
TN = (((0,), (0,)), ((), ()))
SOURCE_Z = (0, -1, 1, -2, 2, -3, 3, 4)


def in_hbm(v):
    return pltpu.with_memory_space_constraint(v, pltpu.HBM)


def in_vmem(v):
    return pltpu.with_memory_space_constraint(v, pltpu.VMEM)


def load_all(pairs, sems):
    copies = [pltpu.make_async_copy(a, b, sems.at[i]) for i, (a, b) in enumerate(pairs)]
    for copy in copies:
        copy.start()
    return copies


def split3(v):
    a = v.astype(BF16)
    r = v - a.astype(F32)
    b = r.astype(BF16)
    c = (r - b.astype(F32)).astype(BF16)
    return jnp.concatenate([a, b, c], axis=0)


def fold3(v):
    n = v.shape[0] // 3
    return v[:n] + v[n : 2 * n] + v[2 * n :]


def first_kernel(x_ref, q_hbm, e_hbm, h_hbm, *refs):
    outs, (q_ref, e_ref, h_ref, sems) = refs[:4], refs[4:]
    columns = [pl.ds(pl.multiple_of((x_ref[0] + s) % 4 * 1024, 1024), 1024) for s in range(4)]
    loads = load_all(
        [(q_hbm, q_ref), (h_hbm, h_ref)]
        + [(e_hbm.at[:, columns[s]], e_ref.at[s]) for s in (1, 3, 2, 0)],
        sems,
    )
    loads[0].wait()
    q = q_ref[...].astype(BF16)
    loads[1].wait()
    t = jnp.dot(q, h_ref[...], preferred_element_type=F32)
    high = t.astype(BF16)
    low = (t - high.astype(F32)).astype(BF16)
    for load, s in zip(loads[2:], (1, 3, 2, 0)):
        load.wait()
        eq = jnp.dot(q, e_ref[s], preferred_element_type=F32)
        outs[s][0:32, :] = high
        outs[s][32:64, :] = low
        outs[s][64:96, :] = eq.astype(BF16)


def first(x_index, q_t, e_t, h_t):
    return pl.pallas_call(
        first_kernel,
        in_specs=[SMEM] + [HBM] * 3,
        out_specs=[VMEM] * 4,
        out_shape=[jax.ShapeDtypeStruct((96, 1024), BF16)] * 4,
        scratch_shapes=[
            pltpu.VMEM((32, 448), F32),
            pltpu.VMEM((4, 448, 1024), BF16),
            pltpu.VMEM((448, 1024), BF16),
            pltpu.SemaphoreType.DMA((6,)),
        ],
        compiler_params=vmem(12),
        name="eq_hq",
    )(x_index, in_hbm(q_t), in_hbm(e_t), in_hbm(h_t))


def products(t, x_ref, slabs):
    out = []
    for pair in range(0, slabs, 2):
        two = [x_ref[1024 * j : 1024 * (j + 1), :] for j in range(pair, min(pair + 2, slabs))]
        p = fold3(jnp.dot(t, jnp.concatenate(two, axis=1), preferred_element_type=F32))
        out += [p[:, 128 * s : 128 * (s + 1)] for s in range(len(two))]
    return out


def column_kernel(z_ref, *refs):
    messages, xs, (out_ref, t_ref, m_ref, x_ref, sems) = refs[:4], refs[4:11], refs[11:]
    loads = load_all(
        [(m, m_ref.at[i]) for i, m in enumerate(messages)]
        + [(v, x_ref.at[pl.ds(1024 * i, 1024), :]) for i, v in enumerate(xs)],
        sems,
    )
    for load in loads[:4]:
        load.wait()
    m = sum(m_ref[i].astype(F32) for i in range(4))
    t = split3(m[0:32] + m[32:64])
    t_ref[...] = t
    for z in range(8):
        out_ref[z] = m[64:96, 128 * z : 128 * (z + 1)]
    for load in loads[4:]:
        load.wait()
    for j, p in enumerate(products(t, x_ref, 7)):
        out_ref[z_ref[j]] += p


def column(z_index, messages, slabs):
    return pl.pallas_call(
        column_kernel,
        in_specs=[SMEM] + [ANY] * 11,
        out_specs=[VMEM] * 2,
        out_shape=[
            jax.ShapeDtypeStruct((8, 32, 128), F32),
            jax.ShapeDtypeStruct((96, 1024), BF16),
        ],
        scratch_shapes=[
            pltpu.VMEM((4, 96, 1024), BF16),
            pltpu.VMEM((7 * 1024, 128), BF16),
            pltpu.SemaphoreType.DMA((11,)),
        ],
        compiler_params=vmem(8),
        name="p_column",
    )(z_index, *messages, *slabs)


def column_rest_kernel(z_ref, part_ref, t_ref, *refs):
    slabs, (out_ref, x_ref, sems) = refs[:1], refs[1:]
    copies = [(v, x_ref.at[pl.ds(1024 * i, 1024), :]) for i, v in enumerate(slabs)]
    loads = load_all(copies, sems)
    out_ref[...] = part_ref[...]
    for load in loads:
        load.wait()
    for j, p in enumerate(products(t_ref[...], x_ref, 1)):
        out_ref[z_ref[7 + j]] += p


def column_rest(z_index, part, t, slabs):
    return pl.pallas_call(
        column_rest_kernel,
        in_specs=[SMEM] + [VMEM] * 2 + [ANY],
        out_specs=VMEM,
        out_shape=jax.ShapeDtypeStruct((8, 32, 128), F32),
        scratch_shapes=[pltpu.VMEM((1024, 128), BF16), pltpu.SemaphoreType.DMA((1,))],
        compiler_params=vmem(6),
        name="p_column_rest",
    )(z_index, part, t, *slabs)


def add_spread_kernel(scale, in_ref, out_ref):
    s = jnp.sum(in_ref[...], axis=0) * scale
    out_ref[...] = jnp.broadcast_to(s[None], out_ref.shape)


def add_spread(v, copies, scale):
    return pl.pallas_call(
        functools.partial(add_spread_kernel, scale),
        in_specs=[VMEM],
        out_specs=VMEM,
        out_shape=jax.ShapeDtypeStruct((copies, *v.shape[1:]), F32),
        compiler_params=vmem(4),
        name="add_spread",
    )(v)


def pack_kernel(*refs):
    parts, (out, sems) = refs[:-2], refs[-2:]
    copies = [(v, out.at[pl.ds(1024 * i, 1024), :]) for i, v in enumerate(parts)]
    for copy in load_all(copies, sems):
        copy.wait()


def pack(arrays):
    return pl.pallas_call(
        pack_kernel,
        in_specs=[ANY] * len(arrays),
        out_specs=HBM,
        out_shape=pltpu.HBM((1024 * len(arrays), 128), BF16),
        scratch_shapes=[pltpu.SemaphoreType.DMA((len(arrays),))],
        compiler_params=vmem(4),
        name="pack",
    )(*arrays)


def slab_copies(at_ref, first, e_hbm, x_hbm, parts_of, e_ref, x_ref):
    slabs = [(r, first_of + i) for r, (first_of, n) in zip(x_hbm, parts_of) for i in range(n)]
    pairs = []
    for place, (r, i) in enumerate(slabs):
        cols = pl.ds(pl.multiple_of(at_ref[first + place] * 128, 128), 128)
        pairs.append((r.at[pl.ds(1024 * i, 1024), :], x_ref.at[place]))
        pairs.append((e_hbm.at[:, cols], e_ref.at[place]))
    return pairs


def correct_pair(pair, loads, h_ref, e_ref, x_ref, out_ref):
    for load in loads[4 * pair : 4 * pair + 4]:
        load.wait()
    x = jnp.concatenate([x_ref[2 * pair], x_ref[2 * pair + 1]], axis=1)
    grad = jnp.dot(h_ref[...], x, preferred_element_type=F32)
    for s in range(2):
        place = 2 * pair + s
        both = e_ref[place].astype(F32) + grad[:, 128 * s : 128 * (s + 1)]
        out_ref[place] = both.astype(BF16)


def correct_kernel(parts_of, at_ref, h_hbm, e_hbm, *refs):
    x_hbm, (out_ref, h_ref, e_ref, x_ref, sems) = refs[:-5], refs[-5:]
    copies = slab_copies(at_ref, 0, e_hbm, x_hbm, parts_of, e_ref, x_ref)
    loads = load_all([(h_hbm, h_ref)] + copies, sems)
    loads[0].wait()
    for pair in range(at_ref.shape[0] // 2):
        correct_pair(pair, loads[1:], h_ref, e_ref, x_ref, out_ref)


def correct_scratch(n):
    return [
        pltpu.VMEM((448, 1024), BF16),
        pltpu.VMEM((n, 448, 128), BF16),
        pltpu.VMEM((n, 1024, 128), BF16),
        pltpu.SemaphoreType.DMA((1 + 2 * n,)),
    ]


def correct(places, h_t, e_t, arrays, parts_of):
    n = places.shape[0]
    return pl.pallas_call(
        functools.partial(correct_kernel, parts_of),
        in_specs=[SMEM] + [HBM] * (2 + len(arrays)),
        out_specs=VMEM,
        out_shape=pltpu.VMEM((n, 448, 128), BF16),
        scratch_shapes=correct_scratch(n),
        compiler_params=vmem(20),
        name="corrected",
    )(places, *[in_hbm(v) for v in [h_t, e_t, *arrays]])


def finish_kernel(kept_count, at_ref, p_ref, *refs):
    kept_refs, (h_hbm, e_hbm), refs = (
        refs[:kept_count],
        refs[kept_count : kept_count + 2],
        refs[kept_count + 2 :],
    )
    x_hbm, (w_ref, out_hbm, h_ref, e_ref, x_ref, sems, out_ref, out_sem) = refs[:-8], refs[-8:]
    rest = len(x_hbm)
    copies = slab_copies(at_ref, 32 - rest, e_hbm, x_hbm, [(0, 1)] * rest, e_ref, x_ref)
    loads = load_all([(h_hbm, h_ref)] + copies, sems)
    slabs = [(r, i) for r in [*kept_refs, out_ref] for i in range(r.shape[0])]

    def project_pair(pair):
        two = (2 * pair, 2 * pair + 1)
        p = jnp.concatenate([p_ref[at_ref[i]] for i in two], axis=1)
        c = jnp.concatenate([slabs[i][0][slabs[i][1]] for i in two], axis=1)
        return lax.dot_general(split3(p), c, NT, preferred_element_type=F32)

    total = sum(project_pair(pair) for pair in range(16 - rest // 2))
    loads[0].wait()
    for pair in range(rest // 2):
        correct_pair(pair, loads[1:], h_ref, e_ref, x_ref, out_ref)
    store = pltpu.make_async_copy(out_ref, out_hbm, out_sem)
    store.start()
    total = total + sum(project_pair(pair) for pair in range(16 - rest // 2, 16))
    w_ref[...] = fold3(total)
    store.wait()


def finish(places, p_blocks, kept, h_t, e_t, rest):
    n = len(rest)
    return pl.pallas_call(
        functools.partial(finish_kernel, len(kept)),
        in_specs=[SMEM] + [VMEM] * (1 + len(kept)) + [HBM] * (2 + n),
        out_specs=[VMEM, HBM],
        out_shape=[jax.ShapeDtypeStruct((32, 448), F32), pltpu.HBM((n, 448, 128), BF16)],
        scratch_shapes=correct_scratch(n)
        + [pltpu.VMEM((n, 448, 128), BF16), pltpu.SemaphoreType.DMA],
        compiler_params=vmem(14),
        name="c_p",
    )(places, p_blocks, *[in_vmem(v) for v in kept], *[in_hbm(v) for v in [h_t, e_t, *rest]])


def load_pieces(kept_refs, hbm, buffer, sem):
    load = pltpu.make_async_copy(hbm, buffer, sem)
    load.start()
    return [(r, i) for r in [*kept_refs, buffer] for i in range(r.shape[0])], load


def factor_kernel(p_ref, inv_ref, p_out_ref, low_ref):
    p = split3(jnp.concatenate([p_ref[i] for i in range(32)], axis=1))
    gram = fold3(lax.dot_general(p, p, NT, preferred_element_type=F32))
    gram = gram[:, 0:32] + gram[:, 32:64] + gram[:, 64:96]
    row = lax.broadcasted_iota(jnp.int32, (32, 128), 0)
    col = lax.broadcasted_iota(jnp.int32, (32, 128), 1)
    work = jnp.concatenate([gram, jnp.zeros((32, 96), F32)], axis=1)
    work = jnp.where(col == row + 32, 1.0, work)
    scale = jnp.zeros((32, 128), F32)
    for start in range(0, 32, 8):
        block = range(start, start + 8)
        columns = {j: jnp.broadcast_to(work[:, j : j + 1], (32, 128)) for j in block}
        for j in block:
            pivot = columns[j][j : j + 1, :]
            scale = jnp.where(row == j, pivot, scale)
            below = jnp.where(row > j, columns[j], 0.0) * (1.0 / pivot)
            work = work - below * work[j : j + 1, :]
            for k in range(j + 1, start + 8):
                columns[k] = columns[k] - below * columns[k][j : j + 1, :]
    inverse = (work / jnp.sqrt(scale))[:, 32:64]
    inv_ref[...] = inverse
    terms = split3(inverse)
    terms = jnp.concatenate([terms, terms, terms], axis=1)
    out = fold3(jnp.dot(terms, p, preferred_element_type=F32))
    p_out_ref[...] = out
    low_ref[...] = out.astype(BF16)


def factor(p_blocks):
    return pl.pallas_call(
        factor_kernel,
        in_specs=[VMEM],
        out_specs=[VMEM] * 3,
        out_shape=[
            jax.ShapeDtypeStruct((32, 32), F32),
            jax.ShapeDtypeStruct((32, 4096), F32),
            jax.ShapeDtypeStruct((32, 4096), BF16),
        ],
        compiler_params=vmem(8),
        name="factor",
    )(p_blocks)


def final_kernel(at_ref, inv_ref, a_ref, b_ref, c_ref, d_ref, low_ref, *refs):
    kept_refs, (c_hbm, q_ref, out_hbm, buffer, stage, sem, out_sems) = refs[:-7], refs[-7:]
    slabs, load = load_pieces(kept_refs, c_hbm, buffer, sem)
    w = (a_ref[...] + b_ref[...] + c_ref[...] + d_ref[...]) * 0.25
    q = jnp.dot(inv_ref[...], w, precision=lax.Precision.HIGHEST, preferred_element_type=F32)
    q_ref[...] = q
    rows = q.T.astype(BF16)
    stores = []
    for pair in range(16):
        if 2 * pair == 32 - buffer.shape[0]:
            load.wait()
        places = [pl.ds(pl.multiple_of(at_ref[2 * pair + s] * 128, 128), 128) for s in range(2)]
        p = jnp.concatenate([low_ref[:, place] for place in places], axis=1)
        approx = jnp.dot(rows, p, preferred_element_type=F32)
        for s, place in enumerate(places):
            i = 2 * pair + s
            kept = slabs[i][0][slabs[i][1]].astype(F32)
            stage[i] = (kept - approx[:, 128 * s : 128 * (s + 1)]).astype(BF16)
            store = pltpu.make_async_copy(stage.at[i], out_hbm.at[:, place], out_sems.at[i])
            store.start()
            stores.append(store)
    for store in stores:
        store.wait()


def final(places, inverse, parts, p_low, kept, piece):
    return pl.pallas_call(
        final_kernel,
        in_specs=[SMEM] + [VMEM] * (6 + len(kept)) + [HBM],
        out_specs=[VMEM, HBM],
        out_shape=[
            jax.ShapeDtypeStruct((32, 448), F32),
            jax.ShapeDtypeStruct((448, 4096), BF16),
        ],
        scratch_shapes=[
            pltpu.VMEM(piece.shape, BF16),
            pltpu.VMEM((32, 448, 128), BF16),
            pltpu.SemaphoreType.DMA,
            pltpu.SemaphoreType.DMA((32,)),
        ],
        compiler_params=vmem(14),
        name="new_error",
    )(places, inverse, *parts, p_low, *[in_vmem(v) for v in kept], in_hbm(piece))


def swap(v, axis="hidden", groups=None):
    return lax.all_to_all(v, axis, 0, 0, axis_index_groups=groups)


def replicas(v):
    return [v] + [
        lax.ppermute(v, "replica", [(i, (i + s) % 4) for i in range(4)]) for s in (1, 3, 2)
    ]


def move(v, dx, dz):
    pairs = [(h, (h // 8 + dx) % 4 * 8 + (h % 8 + dz) % 8) for h in range(32)]
    return lax.ppermute(v, "hidden", pairs)


def together(*values):
    return lax.optimization_barrier(values)


def shards(activations, hidden_grad, error_buffer, q_previous):
    x = activations[0]
    me = lax.axis_index("hidden")
    x_index, z_index = me // 8, me % 8
    z_order = jnp.stack([(z_index + rz) % 8 for rz in SOURCE_Z]).astype(jnp.int32)

    def places(*columns):
        rx = np.concatenate([np.full(len(rz), r) for r, rz in columns]).astype(np.int32)
        rz = np.concatenate([rz for _, rz in columns]).astype(np.int32)
        return ((x_index + rx) % 4 * 8 + (z_index + rz) % 8).astype(jnp.int32)

    e_t, h_t = error_buffer[0, 0].T, hidden_grad[0].T
    mine, *others = first(x_index.astype(jnp.int32)[None], q_previous[0].T, e_t, h_t)
    p1, m1, f0 = move(x, 0, 1), move(x, 0, -1), move(x, 2, 0)
    g1, g2, g3 = [move(m, dx, 0) for m, dx in zip(others, (1, 2, -1))]
    p1, m1, mine = together(p1, m1, mine)
    p2, m2 = move(p1, 0, 1), move(m1, 0, -1)
    p2, m2, f0 = together(p2, m2, f0)
    p3, m3 = move(p2, 0, 1), move(m2, 0, -1)
    fp1, fm1 = move(f0, 0, 1), move(f0, 0, -1)
    bundle = pack([x, p1, m1, p2, m2, p3, m3])
    p3, fp1, fm1 = together(p3, fp1, fm1)
    end = move(p3, 0, 1)
    bundle, g1, g2, g3 = together(bundle, g1, g2, g3)
    near = [move(bundle, 1, 0), move(bundle, -1, 0)]
    near_end = [move(end, 1, 0), move(end, -1, 0)]
    part, t = column(z_order, [mine, g1, g2, g3], [x, p1, m1, p2, m2, p3, m3])
    column_groups = [[8 * i + z for z in range(8)] for i in range(4)]
    p_parts = swap(column_rest(z_order, part, t, [end]), groups=column_groups)
    fp2, fm2 = move(fp1, 0, 1), move(fm1, 0, -1)
    fp3, fm3, f_end = move(fp2, 0, 1), move(fm2, 0, -1), move(fm2, 0, -2)
    p_parts = add_spread(p_parts, 4, 1.0)
    p_parts = add_spread(swap(p_parts, "replica"), 32, 0.25)
    kept_own = correct(places((0, SOURCE_Z)), h_t, e_t, [bundle, end], [(0, 7), (0, 1)])
    p_parts, fp3, fm3, f_end, kept_own = together(p_parts, fp3, fm3, f_end, kept_own)
    far = [f0, fp1, fm1, fp2, fm2, fp3, fm3, f_end]
    p_blocks = swap(p_parts)
    middle = [(-1, SOURCE_Z[:7]), (1, SOURCE_Z[:7]), (2, SOURCE_Z[:4])]
    rest = [(-1, SOURCE_Z[7:]), (1, SOURCE_Z[7:]), (2, SOURCE_Z[4:])]
    at = places((0, SOURCE_Z), *middle, *rest)
    parts_of = [(0, 7), (0, 7)] + [(0, 1)] * 4
    kept_middle = correct(places(*middle), h_t, e_t, [*near, *far[:4]], parts_of)
    kept = [kept_own, kept_middle]
    w_part, piece = finish(at, p_blocks, kept, h_t, e_t, [*near_end, *far[4:]])
    parts = replicas(w_part)
    inverse, p_factor, p_low = factor(p_blocks)
    q_factor, new_error = final(at, inverse, parts, p_low, kept, piece)
    return (p_factor.T[None], q_factor.T[None], new_error.T[None, None])


def solution(mesh):
    in_specs = (
        P("expert", "replica", "hidden"),
        P("expert", "replica", "hidden"),
        P("expert", "replica", None, "hidden"),
        P("expert", "hidden", None),
    )
    out_specs = (
        P("expert", None, None),
        P("expert", "hidden", None),
        P("expert", "replica", None, "hidden"),
    )
    return jax.shard_map(shards, mesh=mesh, in_specs=in_specs, out_specs=out_specs, check_vma=False)
```
